256 devices in a mesh: fsdp: 64 (over z, x, core), tensor: 4 (over y).
Axes of the slice: x: 4, y: 4, z: 8, core: 2. Of those that a mesh axis runs over, the one named last changes fastest.
Arguments:
- grad: bfloat16 [26624, 8192], P('fsdp', 'tensor'), may hold values from -6 to 6
- momentum: float32 [26624, 8192], P('fsdp', 'tensor'), may hold values from -6 to 6
- basis: bfloat16 [8192, 256], P('tensor'), may hold values from -0.0625 to 0.0625
Outputs:
- new_momentum: float32 [26624, 8192], P('fsdp', 'tensor')
- update: bfloat16 [26624, 8192], P('fsdp', 'tensor')
- basis_next: bfloat16 [8192, 256], P('tensor')
The draws below stay inside these ranges and needn't reach their ends.
All inputs are finite; a program needn't handle non-finite values.
Results may differ from the reference program's by a relative error of at most 0.0058.
Values may be sent and summed in bfloat16 or wider, within the bound.
A program may use at most 64 MiB of HBM per device.

```python
import math
import jax
import jax.numpy as jnp
from jax import lax

RANK = 256
ROWS = 26624
COLS = 8192


def shard_levels(key, shape, shards, smallest, top_value):
    factor_of, own = 1.0, jax.random.fold_in(key, 6)
    for axis_at, parts in shards:
        heights = jnp.exp(jax.random.uniform(jax.random.fold_in(own, axis_at), (parts,), jnp.float32, smallest / len(shards), top_value / len(shards)))
        factor_of = factor_of * jnp.repeat(heights, shape[axis_at] // parts).reshape([-1 if axis == axis_at else 1 for axis in range(len(shape))])
    return factor_of


def normal_values(stream_key, extent, spread, limit, cuts=(), dtype=jnp.bfloat16):
    result = spread * jax.random.normal(stream_key, extent, jnp.float32)
    if cuts:
        result = result * shard_levels(stream_key, extent, cuts, -0.22, 0.18)
    return jnp.clip(result, -limit, limit).astype(dtype)


def setup_inputs(seed: int = 0) -> dict:
    key_of = jax.random.split(jax.random.key(seed), 4)
    return {
        "grad": normal_values(key_of[0], (ROWS, COLS), 1.0, 6.0, ((0, 64), (1, 4))),
        "momentum": normal_values(key_of[1], (ROWS, COLS), 1.0, 6.0, ((0, 64), (1, 4)), jnp.float32),
        "basis": normal_values(key_of[2], (COLS, RANK), COLS ** -0.5, 0.0625, ((0, 4),)),
    }


def reference(grad, momentum, basis):
    high = lax.Precision.HIGHEST
    blended = momentum + grad.astype(jnp.float32)
    panel = jnp.dot(blended, basis.astype(jnp.float32), precision=high)
    factor_q, factor_r = jnp.linalg.qr(panel)
    signs = jnp.sign(jnp.diagonal(factor_r))
    ortho = factor_q * signs[None, :]
    projected = lax.dot_general(blended, ortho, (((0,), (0,)), ((), ())), precision=high)
    rounded = lax.optimization_barrier(projected.astype(jnp.bfloat16))
    rounded_f = rounded.astype(jnp.float32)
    new_momentum = blended - 0.05 * jnp.dot(ortho, rounded_f.T, precision=high)
    column_sq = lax.optimization_barrier(jnp.sum(rounded_f * rounded_f, axis=0))
    basis_next = lax.optimization_barrier((rounded_f * lax.rsqrt(column_sq + 1e-06)[None, :]).astype(jnp.bfloat16))
    factor = math.sqrt(ROWS * COLS / RANK)
    update = (factor * jnp.dot(ortho, basis_next.astype(jnp.float32).T, precision=high)).astype(jnp.bfloat16)
    return (new_momentum, update, basis_next)
```

```python
import math

import jax
import jax.numpy as jnp
from jax import lax
from jax.experimental import pallas as pl
from jax.experimental.pallas import tpu as pltpu
from jax.sharding import PartitionSpec as P

HIGH = lax.Precision.HIGHEST
F32 = jnp.float32


def dot(a, b, dims):
    return lax.dot_general(a, b, (dims, ((), ())), precision=HIGH, preferred_element_type=F32)


def inverse_factor(square):
    size = square.shape[0]
    tall = size // 8
    tiles = [square[8 * i : 8 * i + 8, :] for i in range(tall)]
    lane = lax.broadcasted_iota(jnp.int32, (8, size), 1)
    sub = lax.broadcasted_iota(jnp.int32, (8, size), 0)
    pivots = []
    for t in range(tall):
        start = 8 * t
        left = tall - t
        cols = [
            [jnp.broadcast_to(tiles[i][:, start + l : start + l + 1], (8, size)) for i in range(t, tall)]
            for l in range(8)
        ]
        mult = [[None] * left for _ in range(8)]
        group = tiles[t]
        rows = []
        pivot = jnp.zeros((8, size), F32)
        for l in range(8):
            here = cols[l][0][l : l + 1, :]
            recip = jnp.broadcast_to(1.0 / here, (8, size))
            pivot = jnp.where(sub == l, here, pivot)
            mult[l][0] = jnp.where(sub > l, cols[l][0] * recip, 0.0)
            for i in range(1, left):
                mult[l][i] = cols[l][i] * recip
            for later in range(l + 1, 8):
                across = jnp.broadcast_to(cols[later][0][l : l + 1, :], (8, size))
                for i in range(left):
                    cols[later][i] = cols[later][i] - mult[l][i] * across
            at = start + l
            row = jnp.where(lane[:1] == at, 1.0, group[l : l + 1, :])
            group = jnp.where((lane == at) & (sub > l), 0.0, group)
            group = group - mult[l][0] * jnp.broadcast_to(row, (8, size))
            row = jnp.where((lane[:1] > at) & (lane[:1] < start + 8), 0.0, row)
            rows.append(jnp.broadcast_to(row, (8, size)))
        tiles[t] = group
        pivots.append(pivot)
        for i in range(1, left):
            total = mult[0][i] * rows[0]
            for l in range(1, 8):
                total = total + mult[l][i] * rows[l]
            kept = jnp.where((lane >= start) & (lane < start + 8), 0.0, tiles[t + i])
            tiles[t + i] = kept - total
    out = []
    for i in range(tall):
        at = sub + 8 * i
        unit = jnp.where(lane == at, 1.0, jnp.where(lane < at, tiles[i], 0.0))
        out.append(unit * lax.rsqrt(pivots[i]))
    return jnp.concatenate(out, 0)


def factor_kernel(gram_ref, out_ref):
    half = gram_ref.shape[0] // 2
    first = inverse_factor(gram_ref[:half, :half])
    across = dot(first, gram_ref[:half, half:], ((1,), (0,)))
    second = inverse_factor(gram_ref[half:, half:] - dot(across, across, ((0,), (0,))))
    below = -dot(across, first, ((0,), (0,)))
    out_ref[:half, :half] = first
    out_ref[:half, half:] = jnp.zeros((half, half), F32)
    out_ref[half:, :half] = dot(second, below, ((1,), (0,)))
    out_ref[half:, half:] = second


def factor(gram):
    return pl.pallas_call(
        factor_kernel,
        out_shape=jax.ShapeDtypeStruct(gram.shape, F32),
        in_specs=[pl.BlockSpec(memory_space=pltpu.VMEM)],
        out_specs=pl.BlockSpec(memory_space=pltpu.VMEM),
        compiler_params=pltpu.CompilerParams(vmem_limit_bytes=32 << 20),
    )(gram)


def on_device(grad, momentum, basis):
    rows_here, cols_here = grad.shape
    rank = basis.shape[1]
    blended = momentum + grad.astype(F32)
    panel = lax.psum(dot(blended, basis.astype(F32), ((1,), (0,))), "tensor")
    gram = lax.psum(dot(panel, panel, ((0,), (0,))), "fsdp")
    partial = dot(blended, panel, ((0,), (0,)))
    mine = lax.psum_scatter(partial, "fsdp", scatter_dimension=0, tiled=True)
    inverse = factor(gram)
    ortho = dot(panel, inverse, ((1,), (1,)))
    shard = dot(mine, inverse, ((1,), (1,))).astype(jnp.bfloat16)
    rounded = lax.all_gather(shard, "fsdp", axis=0, tiled=True)
    rounded_f = rounded.astype(F32)
    column_sq = lax.psum(jnp.sum(rounded_f * rounded_f, axis=0), "tensor")
    basis_next = (rounded_f * lax.rsqrt(column_sq + 1e-06)[None, :]).astype(jnp.bfloat16)
    ortho_b = ortho.astype(jnp.bfloat16)
    back = lax.dot_general(ortho_b, rounded, (((1,), (1,)), ((), ())), preferred_element_type=F32)
    new_momentum = blended - 0.05 * back
    scale = math.sqrt(rows_here * lax.axis_size("fsdp") * cols_here * lax.axis_size("tensor") / rank)
    step = lax.dot_general(ortho_b, basis_next, (((1,), (1,)), ((), ())), preferred_element_type=F32)
    update = (scale * step).astype(jnp.bfloat16)
    return (new_momentum, update, basis_next)


def solution(mesh):
    return jax.shard_map(
        on_device,
        mesh=mesh,
        in_specs=(P("fsdp", "tensor"), P("fsdp", "tensor"), P("tensor", None)),
        out_specs=(P("fsdp", "tensor"), P("fsdp", "tensor"), P("tensor", None)),
        check_vma=False,
    )
```

```python
import functools
import math

import jax
import jax.numpy as jnp
from jax import lax
from jax.experimental import pallas as pl
from jax.experimental.pallas import tpu as pltpu
from jax.sharding import PartitionSpec as P

MESH = pl.DeviceIdType.MESH
BF16 = jnp.bfloat16
HIGH = lax.Precision.HIGHEST
F32 = jnp.float32


def dot(a, b, dims):
    return lax.dot_general(a, b, (dims, ((), ())), precision=HIGH, preferred_element_type=F32)


def inverse_factor(square):
    size = square.shape[0]
    tall = size // 8
    tiles = [square[8 * i : 8 * i + 8, :] for i in range(tall)]
    lane = lax.broadcasted_iota(jnp.int32, (8, size), 1)
    sub = lax.broadcasted_iota(jnp.int32, (8, size), 0)
    pivots = []
    for t in range(tall):
        start = 8 * t
        left = tall - t
        cols = [
            [jnp.broadcast_to(tiles[i][:, start + l : start + l + 1], (8, size)) for i in range(t, tall)]
            for l in range(8)
        ]
        mult = [[None] * left for _ in range(8)]
        group = tiles[t]
        rows = []
        pivot = jnp.zeros((8, size), F32)
        for l in range(8):
            here = cols[l][0][l : l + 1, :]
            recip = jnp.broadcast_to(1.0 / here, (8, size))
            pivot = jnp.where(sub == l, here, pivot)
            mult[l][0] = jnp.where(sub > l, cols[l][0] * recip, 0.0)
            for i in range(1, left):
                mult[l][i] = cols[l][i] * recip
            for later in range(l + 1, 8):
                across = jnp.broadcast_to(cols[later][0][l : l + 1, :], (8, size))
                for i in range(left):
                    cols[later][i] = cols[later][i] - mult[l][i] * across
            at = start + l
            row = jnp.where(lane[:1] == at, 1.0, group[l : l + 1, :])
            group = jnp.where((lane == at) & (sub > l), 0.0, group)
            group = group - mult[l][0] * jnp.broadcast_to(row, (8, size))
            row = jnp.where((lane[:1] > at) & (lane[:1] < start + 8), 0.0, row)
            rows.append(jnp.broadcast_to(row, (8, size)))
        tiles[t] = group
        pivots.append(pivot)
        for i in range(1, left):
            total = mult[0][i] * rows[0]
            for l in range(1, 8):
                total = total + mult[l][i] * rows[l]
            kept = jnp.where((lane >= start) & (lane < start + 8), 0.0, tiles[t + i])
            tiles[t + i] = kept - total
    out = []
    for i in range(tall):
        at = sub + 8 * i
        unit = jnp.where(lane == at, 1.0, jnp.where(lane < at, tiles[i], 0.0))
        out.append(unit * lax.rsqrt(pivots[i]))
    return jnp.concatenate(out, 0)


def factor_kernel(gram_ref, out_ref):
    half = gram_ref.shape[0] // 2
    first = inverse_factor(gram_ref[:half, :half])
    across = dot(first, gram_ref[:half, half:], ((1,), (0,)))
    second = inverse_factor(gram_ref[half:, half:] - dot(across, across, ((0,), (0,))))
    below = -dot(across, first, ((0,), (0,)))
    out_ref[:half, :half] = first
    out_ref[:half, half:] = jnp.zeros((half, half), F32)
    out_ref[half:, :half] = dot(second, below, ((1,), (0,)))
    out_ref[half:, half:] = second


def fast_dot(a, b, dims):
    return lax.dot_general(a, b, (dims, ((), ())), preferred_element_type=F32)


def two_parts(value):
    upper = value.astype(BF16)
    return upper, (value - upper.astype(F32)).astype(BF16)


def put(src, dst, send, recv, **where):
    copy = pltpu.make_async_remote_copy(
        src_ref=src, dst_ref=dst, send_sem=send, recv_sem=recv, device_id=where, device_id_type=MESH
    )
    copy.start()
    return copy


def place():
    flat = lax.axis_index("fsdp")
    return flat // 8, flat % 8 // 2, flat % 2, lax.axis_index("tensor")


def at(z, x, core):
    return z * 8 + x * 2 + core


def greet(others):
    barrier = pltpu.get_barrier_semaphore()
    for where in others:
        pl.semaphore_signal(barrier, inc=1, device_id=where, device_id_type=MESH)
    return lambda: pl.semaphore_wait(barrier, len(others))


ORDER = (2, 1, 3, 0)


def sums_kernel(
    grad_hbm, momentum_hbm, basis_hbm,
    panel, gram, shard,
    grad_in, momentum_in, basis_in, high, low, piece, panel_got,
    quarter, gram_got, gram_z, cross, cross_got, lane_sent, lane_got, block, block_got,
    load_sem, ysend, yrecv, gsend, grecv, csend, crecv, xsend, xrecv, zsend, zrecv,
):
    z, x, core, y = place()
    b = x * 2 + core
    rows = grad_hbm.shape[0]
    fourth = rows // 4
    taller = fourth + 8
    others = [{"tensor": (y + o) % 4} for o in (1, 2, 3)]
    others += [{"fsdp": z * 8 + (b + o) % 8} for o in range(1, 8)]
    others += [{"fsdp": (z + o) % 8 * 8 + b} for o in range(1, 8)]
    greeted = greet(others)
    basis_load = pltpu.make_async_copy(basis_hbm, basis_in, load_sem.at[8])
    basis_load.start()
    loads = []
    for n, o in enumerate(ORDER):
        p = (y + o) % 4
        start = pl.multiple_of(p * fourth - 8 * (p % 2), 16)
        for which, (src, dst) in enumerate(((grad_hbm, grad_in), (momentum_hbm, momentum_in))):
            load = pltpu.make_async_copy(src.at[pl.ds(start, taller)], dst.at[n], load_sem.at[2 * n + which])
            load.start()
            loads.append(load)
    basis_load.wait()
    copies = []
    for n, o in enumerate(ORDER):
        p = (y + o) % 4
        start = pl.multiple_of(p * fourth - 8 * (p % 2), 16)
        skip = pl.multiple_of(8 * (p % 2), 8)
        loads[2 * n].wait()
        loads[2 * n + 1].wait()
        upper, lower = two_parts(momentum_in[n] + grad_in[n].astype(F32))
        high[pl.ds(start, taller), :] = upper
        low[pl.ds(start, taller), :] = lower
        basis_v = basis_in[...]
        piece[n] = fast_dot(upper, basis_v, ((1,), (0,))) + fast_dot(lower, basis_v, ((1,), (0,)))
        if n == 0:
            greeted()
        if o:
            copies.append(put(piece.at[n, pl.ds(skip, fourth)], panel_got.at[o - 1], ysend.at[o - 1], yrecv.at[o - 1], tensor=p))
    skip = pl.multiple_of(8 * (y % 2), 8)
    total = piece[3, pl.ds(skip, fourth), :]
    for copy in copies:
        copy.wait_recv()
    for o in (1, 2, 3):
        total = total + panel_got[o - 1]
    mine = pl.ds(pl.multiple_of(y * fourth, 8), fourth)
    panel[mine, :] = total
    gathers = [
        put(panel.at[mine], panel.at[mine], ysend.at[2 + o], yrecv.at[2 + o], tensor=(y + o) % 4) for o in (1, 2, 3)
    ]
    for copy in gathers:
        copy.wait_recv()
    copies += gathers

    whole = panel[...]
    wide = panel[:, pl.ds(pl.multiple_of(y // 2 * 128, 128), 128)]
    quarter[...] = dot(wide, whole, ((0,), (0,)))
    first = y % 2 * 64
    rounds = []
    for o in range(1, 8):
        to = (b + o) % 8
        rounds.append(
            put(quarter.at[pl.ds(pl.multiple_of(first + to * 8, 8), 8)], gram_got.at[o - 1],
                gsend.at[0, o - 1], grecv.at[0, o - 1], fsdp=z * 8 + to)
        )

    panel_high, panel_low = two_parts(whole)

    def product(start):
        upper = high[:, pl.ds(pl.multiple_of(start, 256), 256)]
        lower = low[:, pl.ds(pl.multiple_of(start, 256), 256)]
        return (
            fast_dot(upper, panel_high, ((0,), (0,)))
            + fast_dot(lower, panel_high, ((0,), (0,)))
            + fast_dot(upper, panel_low, ((0,), (0,)))
        )

    crossing = []
    for n, o in enumerate(ORDER):
        cross[n] = product((1 - core) * 1024 + (x + o) % 4 * 256)
        crossing.append(put(cross.at[n], cross_got.at[n], csend.at[n], crecv.at[n], fsdp=at(z, x, 1 - core)))

    for copy in rounds:
        copy.wait_recv()
    total = quarter[pl.ds(pl.multiple_of(first + b * 8, 8), 8), :]
    for o in range(1, 8):
        total = total + gram_got[o - 1]
    gram_z[z] = total
    copies += rounds
    rounds = [
        put(gram_z.at[z], gram_z.at[z], gsend.at[1, o - 1], grecv.at[1, o - 1], fsdp=(z + o) % 8 * 8 + b)
        for o in range(1, 8)
    ]

    passing = []
    for n, o in enumerate(ORDER):
        own = product(core * 1024 + (x + o) % 4 * 256)
        crossing[n].wait_recv()
        lane_sent[n] = own + cross_got[n]
        if o:
            passing.append(
                put(lane_sent.at[n], lane_got.at[o - 1], xsend.at[o - 1], xrecv.at[o - 1], fsdp=at(z, (x + o) % 4, core))
            )

    for copy in rounds:
        copy.wait_recv()
    total = gram_z[0]
    for n in range(1, 8):
        total = total + gram_z[n]
    here = pl.ds(pl.multiple_of(y * 64 + b * 8, 8), 8)
    gram[here, :] = total
    copies += rounds
    rounds = [
        put(gram.at[here], gram.at[here], gsend.at[2, o - 1], grecv.at[2, o - 1], fsdp=z * 8 + (b + o) % 8)
        for o in range(1, 8)
    ]
    for copy in rounds:
        copy.wait_recv()
    copies += rounds
    here = pl.ds(pl.multiple_of(y * 64, 64), 64)
    rounds = [
        put(gram.at[here], gram.at[here], gsend.at[3, o - 1], grecv.at[3, o - 1], tensor=(y + o) % 4) for o in (1, 2, 3)
    ]

    for copy in passing:
        copy.wait_recv()
    block[...] = lane_sent[3] + lane_got[0] + lane_got[1] + lane_got[2]
    last = []
    for o in range(1, 8):
        to = (z + o) % 8
        last.append(
            put(block.at[pl.ds(pl.multiple_of(to * 32, 32), 32)], block_got.at[o - 1], zsend.at[o - 1], zrecv.at[o - 1],
                fsdp=at(to, x, core))
        )
    for copy in rounds:
        copy.wait_recv()
    copies += rounds
    for copy in last:
        copy.wait_recv()
    total = block[pl.ds(pl.multiple_of(z * 32, 32), 32), :]
    for n in range(7):
        total = total + block_got[n]
    shard[...] = total
    for copy in copies + crossing + passing + last:
        copy.wait_send()


def sums(grad, momentum, basis):
    rows, cols = grad.shape
    rank = basis.shape[1]
    fourth = rows // 4
    dma = pltpu.SemaphoreType.DMA
    return pl.pallas_call(
        sums_kernel,
        out_shape=(
            jax.ShapeDtypeStruct((rows, rank), F32),
            jax.ShapeDtypeStruct((rank, rank), F32),
            jax.ShapeDtypeStruct((cols // 64, rank), F32),
        ),
        in_specs=[pl.BlockSpec(memory_space=pl.ANY)] * 3,
        out_specs=(pl.BlockSpec(memory_space=pltpu.VMEM),) * 3,
        scratch_shapes=[
            pltpu.VMEM((4, fourth + 8, cols), BF16),
            pltpu.VMEM((4, fourth + 8, cols), F32),
            pltpu.VMEM((cols, rank), BF16),
            pltpu.VMEM((rows, cols), BF16),
            pltpu.VMEM((rows, cols), BF16),
            pltpu.VMEM((4, fourth + 8, rank), F32),
            pltpu.VMEM((3, fourth, rank), F32),
            pltpu.VMEM((128, rank), F32),
            pltpu.VMEM((7, 8, rank), F32),
            pltpu.VMEM((8, 8, rank), F32),
            pltpu.VMEM((4, 256, rank), F32),
            pltpu.VMEM((4, 256, rank), F32),
            pltpu.VMEM((4, 256, rank), F32),
            pltpu.VMEM((3, 256, rank), F32),
            pltpu.VMEM((256, rank), F32),
            pltpu.VMEM((7, 32, rank), F32),
            dma((9,)), dma((6,)), dma((6,)), dma((4, 7)), dma((4, 7)), dma((4,)), dma((4,)),
            dma((3,)), dma((3,)), dma((7,)), dma((7,)),
        ],
        compiler_params=pltpu.CompilerParams(collective_id=0, has_side_effects=True, vmem_limit_bytes=48 << 20),
    )(grad, momentum, basis)


def solve_kernel(gram_ref, panel_ref, shard_ref, ortho_ref, out_ref, inverse):
    factor_kernel(gram_ref, inverse)
    out_ref[...] = dot(shard_ref[...], inverse[...], ((1,), (1,))).astype(BF16)
    ortho_ref[...] = dot(panel_ref[...], inverse[...], ((1,), (1,))).astype(BF16)


def solve(gram, panel, shard):
    return pl.pallas_call(
        solve_kernel,
        out_shape=(jax.ShapeDtypeStruct(panel.shape, BF16), jax.ShapeDtypeStruct(shard.shape, BF16)),
        in_specs=[pl.BlockSpec(memory_space=pltpu.VMEM)] * 3,
        out_specs=(pl.BlockSpec(memory_space=pltpu.VMEM),) * 2,
        scratch_shapes=[pltpu.VMEM(gram.shape, F32)],
        compiler_params=pltpu.CompilerParams(vmem_limit_bytes=32 << 20),
    )(gram, panel, shard)


def gather_kernel(shard, rounded, scales, squares, zsend, zrecv, xsend, xrecv, csend, crecv, ysend, yrecv):
    z, x, core, y = place()
    others = [{"fsdp": at((z + o) % 8, x, core)} for o in range(1, 8)]
    others += [{"fsdp": at(z, (x + o) % 4, core)} for o in (1, 2, 3)]
    others += [{"fsdp": at(z, x, 1 - core)}]
    others += [{"tensor": (y + o) % 4} for o in (1, 2, 3)]
    greeted = greet(others)

    def rows_of(z_of):
        return pl.ds(pl.multiple_of(core * 1024 + x * 256 + z_of * 32, 32), 32)

    rounded[rows_of(z), :] = shard[...]
    greeted()
    here = rows_of(z)
    along_z = [
        put(rounded.at[here], rounded.at[here], zsend.at[o - 1], zrecv.at[o - 1], fsdp=at((z + o) % 8, x, core))
        for o in range(1, 8)
    ]
    along_x = []
    for zo in range(8):
        here = rows_of((z + 8 - zo) % 8)
        if zo:
            along_z[zo - 1].wait_recv()
        for o in (2, 1, 3):
            along_x.append(
                put(rounded.at[here], rounded.at[here], xsend.at[o - 1, zo], xrecv.at[o - 1, zo],
                    fsdp=at(z, (x + o) % 4, core))
            )
    across = []
    for o in (0, 1, 3, 2):
        if o:
            for zo in range(8):
                along_x[3 * zo + (2, 1, 3).index(o)].wait_recv()
        here = pl.ds(pl.multiple_of(core * 1024 + (x + 4 - o) % 4 * 256, 256), 256)
        across.append(put(rounded.at[here], rounded.at[here], csend.at[o], crecv.at[o], fsdp=at(z, x, 1 - core)))
    for copy in across:
        copy.wait_recv()
    total = jnp.zeros((8, rounded.shape[1]), F32)
    for n in range(8):
        part = rounded[256 * n : 256 * n + 256, :].astype(F32)
        part = part * part
        for i in range(32):
            total = total + part[8 * i : 8 * i + 8, :]
    squares[y] = total
    along_y = [
        put(squares.at[y], squares.at[y], ysend.at[o - 1], yrecv.at[o - 1], tensor=(y + o) % 4) for o in (1, 2, 3)
    ]
    for copy in along_y:
        copy.wait_recv()
    total = squares[0] + squares[1] + squares[2] + squares[3]
    total = jnp.sum(total, axis=0, keepdims=True)
    scales[...] = jnp.broadcast_to(lax.rsqrt(total + 1e-06), scales.shape)
    for copy in along_z + along_x + across + along_y:
        copy.wait_send()


def gather(shard):
    rank = shard.shape[1]
    dma = pltpu.SemaphoreType.DMA
    return pl.pallas_call(
        gather_kernel,
        out_shape=(
            jax.ShapeDtypeStruct((64 * shard.shape[0], rank), BF16),
            jax.ShapeDtypeStruct((8, rank), F32),
        ),
        in_specs=[pl.BlockSpec(memory_space=pltpu.VMEM)],
        out_specs=(pl.BlockSpec(memory_space=pltpu.VMEM),) * 2,
        scratch_shapes=[
            pltpu.VMEM((4, 8, rank), F32),
            dma((7,)), dma((7,)), dma((3, 8)), dma((3, 8)), dma((4,)), dma((4,)), dma((3,)), dma((3,)),
        ],
        compiler_params=pltpu.CompilerParams(collective_id=1, has_side_effects=True, vmem_limit_bytes=32 << 20),
    )(shard)


def finish_kernel(scale, grad, momentum, ortho, rounded, scales, new_momentum, update, basis_next):
    columns = rounded[...]
    following = (columns.astype(F32) * scales[:1, :]).astype(BF16)
    basis_next[...] = following
    blended = momentum[...] + grad[...].astype(F32)
    new_momentum[...] = blended - 0.05 * fast_dot(ortho[...], columns, ((1,), (1,)))
    update[...] = (scale * fast_dot(ortho[...], following, ((1,), (1,)))).astype(BF16)


def finish(scale, grad, momentum, ortho, rounded, scales):
    rows, cols = grad.shape
    rank = ortho.shape[1]
    wide = 256
    part = pl.BlockSpec((rows, wide), lambda i: (0, i))
    tall = pl.BlockSpec((wide, rank), lambda i: (i, 0))
    return pl.pallas_call(
        functools.partial(finish_kernel, scale),
        grid=(cols // wide,),
        out_shape=(
            jax.ShapeDtypeStruct((rows, cols), F32),
            jax.ShapeDtypeStruct((rows, cols), BF16),
            jax.ShapeDtypeStruct((cols, rank), BF16),
        ),
        in_specs=[
            part, part, pl.BlockSpec((rows, rank), lambda i: (0, 0)), tall, pl.BlockSpec((8, rank), lambda i: (0, 0)),
        ],
        out_specs=(part, part, tall),
        compiler_params=pltpu.CompilerParams(vmem_limit_bytes=32 << 20),
    )(grad, momentum, ortho, rounded, scales)


def on_device(grad, momentum, basis):
    rows_here, cols_here = grad.shape
    scale = math.sqrt(rows_here * lax.axis_size("fsdp") * cols_here * lax.axis_size("tensor") / basis.shape[1])
    panel, gram, shard = sums(grad, momentum, basis)
    ortho, shard = solve(gram, panel, shard)
    rounded, scales = gather(shard)
    return finish(scale, grad, momentum, ortho, rounded, scales)


def solution(mesh):
    return jax.shard_map(
        on_device,
        mesh=mesh,
        in_specs=(P("fsdp", "tensor"), P("fsdp", "tensor"), P("tensor", None)),
        out_specs=(P("fsdp", "tensor"), P("fsdp", "tensor"), P("tensor", None)),
        check_vma=False,
    )
```

```python
import functools
import math

import jax
import jax.numpy as jnp
from jax import lax
from jax.experimental import pallas as pl
from jax.experimental.pallas import tpu as pltpu
from jax.sharding import PartitionSpec as P

MESH = pl.DeviceIdType.MESH
BF16 = jnp.bfloat16
HIGH = lax.Precision.HIGHEST
F32 = jnp.float32


def dot(a, b, dims):
    return lax.dot_general(a, b, (dims, ((), ())), precision=HIGH, preferred_element_type=F32)


def inverse_factor(square):
    size = square.shape[0]
    tall = size // 8
    tiles = [square[8 * i : 8 * i + 8, :] for i in range(tall)]
    lane = lax.broadcasted_iota(jnp.int32, (8, size), 1)
    sub = lax.broadcasted_iota(jnp.int32, (8, size), 0)
    pivots = []
    for t in range(tall):
        start = 8 * t
        left = tall - t
        cols = [
            [jnp.broadcast_to(tiles[i][:, start + l : start + l + 1], (8, size)) for i in range(t, tall)]
            for l in range(8)
        ]
        mult = [[None] * left for _ in range(8)]
        group = tiles[t]
        rows = []
        pivot = jnp.zeros((8, size), F32)
        for l in range(8):
            here = cols[l][0][l : l + 1, :]
            recip = jnp.broadcast_to(1.0 / here, (8, size))
            pivot = jnp.where(sub == l, here, pivot)
            mult[l][0] = jnp.where(sub > l, cols[l][0] * recip, 0.0)
            for i in range(1, left):
                mult[l][i] = cols[l][i] * recip
            for later in range(l + 1, 8):
                across = jnp.broadcast_to(cols[later][0][l : l + 1, :], (8, size))
                for i in range(left):
                    cols[later][i] = cols[later][i] - mult[l][i] * across
            at = start + l
            row = jnp.where(lane[:1] == at, 1.0, group[l : l + 1, :])
            group = jnp.where((lane == at) & (sub > l), 0.0, group)
            group = group - mult[l][0] * jnp.broadcast_to(row, (8, size))
            row = jnp.where((lane[:1] > at) & (lane[:1] < start + 8), 0.0, row)
            rows.append(jnp.broadcast_to(row, (8, size)))
        tiles[t] = group
        pivots.append(pivot)
        for i in range(1, left):
            total = mult[0][i] * rows[0]
            for l in range(1, 8):
                total = total + mult[l][i] * rows[l]
            kept = jnp.where((lane >= start) & (lane < start + 8), 0.0, tiles[t + i])
            tiles[t + i] = kept - total
    out = []
    for i in range(tall):
        at = sub + 8 * i
        unit = jnp.where(lane == at, 1.0, jnp.where(lane < at, tiles[i], 0.0))
        out.append(unit * lax.rsqrt(pivots[i]))
    return jnp.concatenate(out, 0)


def factor_kernel(gram_ref, out_ref):
    half = gram_ref.shape[0] // 2
    first = inverse_factor(gram_ref[:half, :half])
    across = dot(first, gram_ref[:half, half:], ((1,), (0,)))
    second = inverse_factor(gram_ref[half:, half:] - dot(across, across, ((0,), (0,))))
    below = -dot(across, first, ((0,), (0,)))
    out_ref[:half, :half] = first
    out_ref[:half, half:] = jnp.zeros((half, half), F32)
    out_ref[half:, :half] = dot(second, below, ((1,), (0,)))
    out_ref[half:, half:] = second


def fast_dot(a, b, dims):
    return lax.dot_general(a, b, (dims, ((), ())), preferred_element_type=F32)


def two_parts(value):
    upper = value.astype(BF16)
    return upper, (value - upper.astype(F32)).astype(BF16)


def put(src, dst, send, recv, **where):
    copy = pltpu.make_async_remote_copy(
        src_ref=src, dst_ref=dst, send_sem=send, recv_sem=recv, device_id=where, device_id_type=MESH
    )
    copy.start()
    return copy


def place():
    flat = lax.axis_index("fsdp")
    return flat // 8, flat % 8 // 2, flat % 2, lax.axis_index("tensor")


def at(z, x, core):
    return z * 8 + x * 2 + core


def greet(others):
    barrier = pltpu.get_barrier_semaphore()
    for where in others:
        pl.semaphore_signal(barrier, inc=1, device_id=where, device_id_type=MESH)
    return lambda: pl.semaphore_wait(barrier, len(others))


ORDER = (2, 1, 3, 0)
ALONG_YX = tuple((oy, ox) for oy in range(4) for ox in range(4) if oy or ox)


def main_kernel(
    grad_hbm, momentum_hbm, basis_hbm,
    rounded, ortho, scales,
    grad_in, momentum_in, basis_in, high, low, piece, panel_got, panel,
    gram_own, gram_half, gram_got, gram_z, gram, inverse,
    cross, cross_got, lane_sent, lane_got, block, block_got, squares, halves,
    load_sem, ysend, yrecv, gsend, grecv, zgsend, zgrecv, g2send, g2recv, g3send, g3recv,
    csend, crecv, xsend, xrecv, zsend, zrecv, azsend, azrecv, axsend, axrecv, acsend, acrecv, sqsend, sqrecv,
):
    z, x, core, y = place()
    rows = grad_hbm.shape[0]
    fourth = rows // 4
    taller = fourth + 8
    sibling = at(z, x, 1 - core)
    others = [{"fsdp": at((z + o) % 8, x, core)} for o in range(1, 8)]
    others += [{"fsdp": at(z, (x + ox) % 4, core), "tensor": (y + oy) % 4} for oy, ox in ALONG_YX]
    others += [{"fsdp": sibling}]
    greeted = greet(others)
    basis_load = pltpu.make_async_copy(basis_hbm, basis_in, load_sem.at[8])
    basis_load.start()
    loads = []
    for n, o in enumerate(ORDER):
        p = (y + o) % 4
        start = pl.multiple_of(p * fourth - 8 * (p % 2), 16)
        for which, (src, dst) in enumerate(((grad_hbm, grad_in), (momentum_hbm, momentum_in))):
            load = pltpu.make_async_copy(src.at[pl.ds(start, taller)], dst.at[n], load_sem.at[2 * n + which])
            load.start()
            loads.append(load)
    basis_load.wait()
    sent = []

    def send(src, dst, send_sem, recv_sem, **where):
        copy = put(src, dst, send_sem, recv_sem, **where)
        sent.append(copy)
        return copy

    copies = []
    for n, o in enumerate(ORDER):
        p = (y + o) % 4
        start = pl.multiple_of(p * fourth - 8 * (p % 2), 16)
        skip = pl.multiple_of(8 * (p % 2), 8)
        loads[2 * n].wait()
        loads[2 * n + 1].wait()
        upper, lower = two_parts(momentum_in[n] + grad_in[n].astype(F32))
        high[pl.ds(start, taller), :] = upper
        low[pl.ds(start, taller), :] = lower
        basis_v = basis_in[...]
        piece[n] = fast_dot(upper, basis_v, ((1,), (0,))) + fast_dot(lower, basis_v, ((1,), (0,)))
        if n == 0:
            greeted()
        if o:
            copies.append(send(piece.at[n, pl.ds(skip, fourth)], panel_got.at[o - 1], ysend.at[o - 1], yrecv.at[o - 1], tensor=p))
    skip = pl.multiple_of(8 * (y % 2), 8)
    total = piece[3, pl.ds(skip, fourth), :]
    for copy in copies:
        copy.wait_recv()
    for o in (1, 2, 3):
        total = total + panel_got[o - 1]
    mine = pl.ds(pl.multiple_of(y * fourth, 8), fourth)
    panel[mine, :] = total
    gathers = [
        send(panel.at[mine], panel.at[mine], ysend.at[2 + o], yrecv.at[2 + o], tensor=(y + o) % 4) for o in (1, 2, 3)
    ]

    half = 128
    gram_own[...] = dot(total, total, ((0,), (0,)))
    away = send(gram_own.at[pl.ds(pl.multiple_of((1 - core) * half, half), half)], gram_half, g3send.at[0], g3recv.at[0], fsdp=sibling)
    away.wait_recv()
    kept = pl.ds(pl.multiple_of(core * half, half), half)
    gram_half[...] = gram_half[...] + gram_own[kept, :]
    spread = []
    for n, (oy, ox) in enumerate(ALONG_YX):
        ty, tx = (y + oy) % 4, (x + ox) % 4
        src = gram_half.at[pl.ds(pl.multiple_of((ty * 4 + tx) * 8, 8), 8)]
        spread.append(send(src, gram_got.at[n], gsend.at[n], grecv.at[n], fsdp=at(z, tx, core), tensor=ty))
    for copy in spread:
        copy.wait_recv()
    eight = (y * 4 + x) * 8
    total = gram_half[pl.ds(pl.multiple_of(eight, 8), 8), :]
    for n in range(15):
        total = total + gram_got[n]
    gram_z[z] = total
    around = [
        send(gram_z.at[z], gram_z.at[z], zgsend.at[o - 1], zgrecv.at[o - 1], fsdp=at((z + o) % 8, x, core))
        for o in range(1, 8)
    ]

    for copy in gathers:
        copy.wait_recv()
    panel_high, panel_low = two_parts(panel[...])

    def product(start):
        upper = high[:, pl.ds(pl.multiple_of(start, 256), 256)]
        lower = low[:, pl.ds(pl.multiple_of(start, 256), 256)]
        return (
            fast_dot(upper, panel_high, ((0,), (0,)))
            + fast_dot(lower, panel_high, ((0,), (0,)))
            + fast_dot(upper, panel_low, ((0,), (0,)))
        )

    crossing = []
    for n, o in enumerate(ORDER):
        cross[n] = product((1 - core) * 1024 + (x + o) % 4 * 256)
        crossing.append(send(cross.at[n], cross_got.at[n], csend.at[n], crecv.at[n], fsdp=sibling))
    passing = []
    for n, o in enumerate(ORDER):
        own = product(core * 1024 + (x + o) % 4 * 256)
        crossing[n].wait_recv()
        own = own + cross_got[n]
        if o:
            lane_sent[n] = own.astype(BF16)
            passing.append(
                send(lane_sent.at[n], lane_got.at[o - 1], xsend.at[o - 1], xrecv.at[o - 1], fsdp=at(z, (x + o) % 4, core))
            )
        else:
            block[...] = own

    for copy in around:
        copy.wait_recv()
    total = gram_z[0]
    for n in range(1, 8):
        total = total + gram_z[n]
    here = pl.ds(pl.multiple_of(core * half + eight, 8), 8)
    gram[here, :] = total
    spread = [
        send(gram.at[here], gram.at[here], g2send.at[n], g2recv.at[n], fsdp=at(z, (x + ox) % 4, core), tensor=(y + oy) % 4)
        for n, (oy, ox) in enumerate(ALONG_YX)
    ]
    for copy in spread:
        copy.wait_recv()
    away = send(gram.at[kept], gram.at[kept], g3send.at[1], g3recv.at[1], fsdp=sibling)

    for copy in passing:
        copy.wait_recv()
    block[...] = block[...] + lane_got[0].astype(F32) + lane_got[1].astype(F32) + lane_got[2].astype(F32)
    last = []
    for o in range(1, 8):
        to = (z + o) % 8
        last.append(
            send(block.at[pl.ds(pl.multiple_of(to * 32, 32), 32)], block_got.at[o - 1], zsend.at[o - 1], zrecv.at[o - 1],
                 fsdp=at(to, x, core))
        )
    away.wait_recv()
    factor_kernel(gram, inverse)
    for copy in last:
        copy.wait_recv()
    total = block[pl.ds(pl.multiple_of(z * 32, 32), 32), :]
    for n in range(7):
        total = total + block_got[n]

    def rows_of(z_of):
        return pl.ds(pl.multiple_of(core * 1024 + x * 256 + z_of * 32, 32), 32)

    here = rows_of(z)
    rounded[here, :] = dot(total, inverse[...], ((1,), (1,))).astype(BF16)
    along_z = [
        send(rounded.at[here], rounded.at[here], azsend.at[o - 1], azrecv.at[o - 1], fsdp=at((z + o) % 8, x, core))
        for o in range(1, 8)
    ]
    along_x = [[None] * 8 for _ in range(4)]

    def pass_on(zo):
        here = rows_of((z + 8 - zo) % 8)
        for o in (2, 1, 3):
            along_x[o][zo] = send(
                rounded.at[here], rounded.at[here], axsend.at[o - 1, zo], axrecv.at[o - 1, zo], fsdp=at(z, (x + o) % 4, core)
            )

    pass_on(0)
    ortho[...] = dot(panel[...], inverse[...], ((1,), (1,))).astype(BF16)
    for zo in (1, 7, 2, 6, 3, 5, 4):
        along_z[zo - 1].wait_recv()
        pass_on(zo)

    def block_of(o):
        return pl.ds(pl.multiple_of(core * 1024 + (x + 4 - o) % 4 * 256, 256), 256)

    across = [send(rounded.at[block_of(0)], rounded.at[block_of(0)], acsend.at[0], acrecv.at[0], fsdp=sibling)]
    total = jnp.zeros((8, rounded.shape[1]), F32)
    part = rounded[block_of(0), :].astype(F32)
    part = part * part
    for i in range(32):
        total = total + part[8 * i : 8 * i + 8, :]
    slot = y * 4 + x
    squares[slot] = total
    spread = [
        send(squares.at[slot], squares.at[slot], sqsend.at[n], sqrecv.at[n], fsdp=at(z, (x + ox) % 4, core), tensor=(y + oy) % 4)
        for n, (oy, ox) in enumerate(ALONG_YX)
    ]
    for copy in spread:
        copy.wait_recv()
    total = squares[0]
    for n in range(1, 16):
        total = total + squares[n]
    halves[core] = total
    away = send(halves.at[core], halves.at[core], g3send.at[2], g3recv.at[2], fsdp=sibling)
    for o in (1, 3, 2):
        for copy in along_x[o]:
            copy.wait_recv()
        across.append(send(rounded.at[block_of(o)], rounded.at[block_of(o)], acsend.at[o], acrecv.at[o], fsdp=sibling))
    away.wait_recv()
    total = jnp.sum(halves[0] + halves[1], axis=0, keepdims=True)
    scales[...] = jnp.broadcast_to(lax.rsqrt(total + 1e-06), scales.shape)
    for copy in across:
        copy.wait_recv()
    for copy in sent:
        copy.wait_send()


def main(grad, momentum, basis):
    rows, cols = grad.shape
    rank = basis.shape[1]
    fourth = rows // 4
    dma = pltpu.SemaphoreType.DMA
    vmem = pltpu.VMEM
    pairs = ((6,), (15,), (7,), (15,), (3,), (4,), (3,), (7,), (7,), (3, 8), (4,), (15,))
    return pl.pallas_call(
        main_kernel,
        out_shape=(
            jax.ShapeDtypeStruct((cols, rank), BF16),
            jax.ShapeDtypeStruct((rows, rank), BF16),
            jax.ShapeDtypeStruct((8, rank), F32),
        ),
        in_specs=[pl.BlockSpec(memory_space=pltpu.HBM)] * 3,
        out_specs=(pl.BlockSpec(memory_space=pltpu.VMEM),) * 3,
        scratch_shapes=[
            vmem((4, fourth + 8, cols), BF16),
            vmem((4, fourth + 8, cols), F32),
            vmem((cols, rank), BF16),
            vmem((rows, cols), BF16),
            vmem((rows, cols), BF16),
            vmem((4, fourth + 8, rank), F32),
            vmem((3, fourth, rank), F32),
            vmem((rows, rank), F32),
            vmem((rank, rank), F32),
            vmem((rank // 2, rank), F32),
            vmem((15, 8, rank), F32),
            vmem((8, 8, rank), F32),
            vmem((rank, rank), F32),
            vmem((rank, rank), F32),
            vmem((4, 256, rank), F32),
            vmem((4, 256, rank), F32),
            vmem((3, 256, rank), BF16),
            vmem((3, 256, rank), BF16),
            vmem((256, rank), F32),
            vmem((7, 32, rank), F32),
            vmem((16, 8, rank), F32),
            vmem((2, 8, rank), F32),
            dma((9,)),
            *[dma(shape) for shape in pairs for _ in range(2)],
        ],
        compiler_params=pltpu.CompilerParams(collective_id=0, has_side_effects=True, vmem_limit_bytes=60 << 20),
    )(grad, momentum, basis)


def finish_kernel(scale, grad, momentum, ortho, rounded, scales, new_momentum, update, basis_next):
    columns = rounded[...]
    following = (columns.astype(F32) * scales[:1, :]).astype(BF16)
    basis_next[...] = following
    blended = momentum[...] + grad[...].astype(F32)
    new_momentum[...] = blended - 0.05 * fast_dot(ortho[...], columns, ((1,), (1,)))
    update[...] = (scale * fast_dot(ortho[...], following, ((1,), (1,)))).astype(BF16)


def finish(scale, grad, momentum, ortho, rounded, scales):
    rows, cols = grad.shape
    rank = ortho.shape[1]
    wide = 256
    part = pl.BlockSpec((rows, wide), lambda i: (0, i))
    tall = pl.BlockSpec((wide, rank), lambda i: (i, 0))
    return pl.pallas_call(
        functools.partial(finish_kernel, scale),
        grid=(cols // wide,),
        out_shape=(
            jax.ShapeDtypeStruct((rows, cols), F32),
            jax.ShapeDtypeStruct((rows, cols), BF16),
            jax.ShapeDtypeStruct((cols, rank), BF16),
        ),
        in_specs=[
            part, part, pl.BlockSpec((rows, rank), lambda i: (0, 0)), tall, pl.BlockSpec((8, rank), lambda i: (0, 0)),
        ],
        out_specs=(part, part, tall),
        compiler_params=pltpu.CompilerParams(vmem_limit_bytes=32 << 20),
    )(grad, momentum, ortho, rounded, scales)


def on_device(grad, momentum, basis):
    rows_here, cols_here = grad.shape
    scale = math.sqrt(rows_here * lax.axis_size("fsdp") * cols_here * lax.axis_size("tensor") / basis.shape[1])
    rounded, ortho, scales = main(grad, momentum, basis)
    return finish(scale, grad, momentum, ortho, rounded, scales)


def solution(mesh):
    return jax.shard_map(
        on_device,
        mesh=mesh,
        in_specs=(P("fsdp", "tensor"), P("fsdp", "tensor"), P("tensor", None)),
        out_specs=(P("fsdp", "tensor"), P("fsdp", "tensor"), P("tensor", None)),
        check_vma=False,
    )
```

```python
import functools
import math

import jax
import jax.numpy as jnp
from jax import lax
from jax.experimental import pallas as pl
from jax.experimental.pallas import tpu as pltpu
from jax.sharding import PartitionSpec as P

MESH = pl.DeviceIdType.MESH
BF16 = jnp.bfloat16
HIGH = lax.Precision.HIGHEST
F32 = jnp.float32


def dot(a, b, dims):
    return lax.dot_general(a, b, (dims, ((), ())), precision=HIGH, preferred_element_type=F32)


def inverse_factor(square):
    size = square.shape[0]
    tall = size // 8
    tiles = [square[8 * i : 8 * i + 8, :] for i in range(tall)]
    lane = lax.broadcasted_iota(jnp.int32, (8, size), 1)
    sub = lax.broadcasted_iota(jnp.int32, (8, size), 0)
    pivots = []
    for t in range(tall):
        start = 8 * t
        left = tall - t
        cols = [
            [jnp.broadcast_to(tiles[i][:, start + l : start + l + 1], (8, size)) for i in range(t, tall)]
            for l in range(8)
        ]
        mult = [[None] * left for _ in range(8)]
        group = tiles[t]
        rows = []
        pivot = jnp.zeros((8, size), F32)
        for l in range(8):
            here = cols[l][0][l : l + 1, :]
            recip = jnp.broadcast_to(1.0 / here, (8, size))
            pivot = jnp.where(sub == l, here, pivot)
            mult[l][0] = jnp.where(sub > l, cols[l][0] * recip, 0.0)
            for i in range(1, left):
                mult[l][i] = cols[l][i] * recip
            for later in range(l + 1, 8):
                across = jnp.broadcast_to(cols[later][0][l : l + 1, :], (8, size))
                for i in range(left):
                    cols[later][i] = cols[later][i] - mult[l][i] * across
            at = start + l
            row = jnp.where(lane[:1] == at, 1.0, group[l : l + 1, :])
            group = jnp.where((lane == at) & (sub > l), 0.0, group)
            group = group - mult[l][0] * jnp.broadcast_to(row, (8, size))
            row = jnp.where((lane[:1] > at) & (lane[:1] < start + 8), 0.0, row)
            rows.append(jnp.broadcast_to(row, (8, size)))
        tiles[t] = group
        pivots.append(pivot)
        for i in range(1, left):
            total = mult[0][i] * rows[0]
            for l in range(1, 8):
                total = total + mult[l][i] * rows[l]
            kept = jnp.where((lane >= start) & (lane < start + 8), 0.0, tiles[t + i])
            tiles[t + i] = kept - total
    out = []
    for i in range(tall):
        at = sub + 8 * i
        unit = jnp.where(lane == at, 1.0, jnp.where(lane < at, tiles[i], 0.0))
        out.append(unit * lax.rsqrt(pivots[i]))
    return jnp.concatenate(out, 0)


def factor_kernel(gram_ref, out_ref):
    half = gram_ref.shape[0] // 2
    first = inverse_factor(gram_ref[:half, :half])
    across = dot(first, gram_ref[:half, half:], ((1,), (0,)))
    second = inverse_factor(gram_ref[half:, half:] - dot(across, across, ((0,), (0,))))
    below = -dot(across, first, ((0,), (0,)))
    out_ref[:half, :half] = first
    out_ref[:half, half:] = jnp.zeros((half, half), F32)
    out_ref[half:, :half] = dot(second, below, ((1,), (0,)))
    out_ref[half:, half:] = second


def fast_dot(a, b, dims):
    return lax.dot_general(a, b, (dims, ((), ())), preferred_element_type=F32)


def two_parts(value):
    upper = value.astype(BF16)
    return upper, (value - upper.astype(F32)).astype(BF16)


def put(src, dst, send, recv, **where):
    copy = pltpu.make_async_remote_copy(
        src_ref=src, dst_ref=dst, send_sem=send, recv_sem=recv, device_id=where, device_id_type=MESH
    )
    copy.start()
    return copy


def place():
    flat = lax.axis_index("fsdp")
    return flat // 8, flat % 8 // 2, flat % 2, lax.axis_index("tensor")


def at(z, x, core):
    return z * 8 + x * 2 + core


def greet(others):
    barrier = pltpu.get_barrier_semaphore()
    for where in others:
        pl.semaphore_signal(barrier, inc=1, device_id=where, device_id_type=MESH)
    return lambda: pl.semaphore_wait(barrier, len(others))


ORDER = (2, 1, 3, 0)
ALONG_YX = tuple((oy, ox) for oy in range(4) for ox in range(4) if oy or ox)


def main_kernel(
    grad_hbm, momentum_hbm, basis_hbm,
    new_momentum, rounded, ortho, scales,
    grad_in, momentum_in, basis_in, high, low, high_turned, low_turned, piece, panel_got, panel,
    gram_own, gram_half, gram_got, gram_z, gram, inverse,
    cross, cross_got, lane_sent, lane_got, block, block_got, squares, halves,
    load_sem, ysend, yrecv, gsend, grecv, zgsend, zgrecv, g2send, g2recv, g3send, g3recv,
    csend, crecv, xsend, xrecv, zsend, zrecv, azsend, azrecv, axsend, axrecv, acsend, acrecv, sqsend, sqrecv,
):
    z, x, core, y = place()
    rows = grad_hbm.shape[0]
    fourth = rows // 4
    taller = fourth + 8
    sibling = at(z, x, 1 - core)
    others = [{"fsdp": at((z + o) % 8, x, core)} for o in range(1, 8)]
    others += [{"fsdp": at(z, (x + ox) % 4, core), "tensor": (y + oy) % 4} for oy, ox in ALONG_YX]
    others += [{"fsdp": sibling}]
    greeted = greet(others)
    basis_load = pltpu.make_async_copy(basis_hbm, basis_in, load_sem.at[8])
    basis_load.start()
    loads = []
    for n, o in enumerate(ORDER):
        p = (y + o) % 4
        start = pl.multiple_of(p * fourth - 8 * (p % 2), 16)
        for which, (src, dst) in enumerate(((grad_hbm, grad_in), (momentum_hbm, momentum_in))):
            load = pltpu.make_async_copy(src.at[pl.ds(start, taller)], dst.at[n], load_sem.at[2 * n + which])
            load.start()
            loads.append(load)
    basis_load.wait()
    sent = []

    def send(src, dst, send_sem, recv_sem, **where):
        copy = put(src, dst, send_sem, recv_sem, **where)
        sent.append(copy)
        return copy

    copies = []
    for n, o in enumerate(ORDER):
        p = (y + o) % 4
        start = pl.multiple_of(p * fourth - 8 * (p % 2), 16)
        skip = pl.multiple_of(8 * (p % 2), 8)
        loads[2 * n].wait()
        loads[2 * n + 1].wait()
        upper, lower = two_parts(momentum_in[n] + grad_in[n].astype(F32))
        high[pl.ds(start, taller), :] = upper
        low[pl.ds(start, taller), :] = lower
        basis_v = basis_in[...]
        piece[n] = fast_dot(upper, basis_v, ((1,), (0,))) + fast_dot(lower, basis_v, ((1,), (0,)))
        if n == 0:
            greeted()
        if o:
            copies.append(send(piece.at[n, pl.ds(skip, fourth)], panel_got.at[o - 1], ysend.at[o - 1], yrecv.at[o - 1], tensor=p))
    for n in range(8):
        wide = slice(256 * n, 256 * n + 256)
        high_turned[wide, :] = high[:, wide].T
        low_turned[wide, :] = low[:, wide].T
    skip = pl.multiple_of(8 * (y % 2), 8)
    total = piece[3, pl.ds(skip, fourth), :]
    for copy in copies:
        copy.wait_recv()
    for o in (1, 2, 3):
        total = total + panel_got[o - 1]
    mine = pl.ds(pl.multiple_of(y * fourth, 8), fourth)
    panel[mine, :] = total
    gathers = [
        send(panel.at[mine], panel.at[mine], ysend.at[2 + o], yrecv.at[2 + o], tensor=(y + o) % 4) for o in (1, 2, 3)
    ]

    half = 128
    gram_own[...] = dot(total, total, ((0,), (0,)))
    away = send(gram_own.at[pl.ds(pl.multiple_of((1 - core) * half, half), half)], gram_half, g3send.at[0], g3recv.at[0], fsdp=sibling)
    away.wait_recv()
    kept = pl.ds(pl.multiple_of(core * half, half), half)
    gram_half[...] = gram_half[...] + gram_own[kept, :]
    spread = []
    for n, (oy, ox) in enumerate(ALONG_YX):
        ty, tx = (y + oy) % 4, (x + ox) % 4
        src = gram_half.at[pl.ds(pl.multiple_of((ty * 4 + tx) * 8, 8), 8)]
        spread.append(send(src, gram_got.at[n], gsend.at[n], grecv.at[n], fsdp=at(z, tx, core), tensor=ty))
    for copy in gathers:
        copy.wait_recv()
    panel_high, panel_low = two_parts(panel[...])

    def product(start):
        upper = high_turned[pl.ds(pl.multiple_of(start, 256), 256), :]
        lower = low_turned[pl.ds(pl.multiple_of(start, 256), 256), :]
        return (
            fast_dot(upper, panel_high, ((1,), (0,)))
            + fast_dot(lower, panel_high, ((1,), (0,)))
            + fast_dot(upper, panel_low, ((1,), (0,)))
        )

    crossing = []
    for n, o in enumerate(ORDER):
        cross[n] = product((1 - core) * 1024 + (x + o) % 4 * 256)
        crossing.append(send(cross.at[n], cross_got.at[n], csend.at[n], crecv.at[n], fsdp=sibling))
    for copy in spread:
        copy.wait_recv()
    eight = (y * 4 + x) * 8
    total = gram_half[pl.ds(pl.multiple_of(eight, 8), 8), :]
    for n in range(15):
        total = total + gram_got[n]
    gram_z[z] = total
    around = [
        send(gram_z.at[z], gram_z.at[z], zgsend.at[o - 1], zgrecv.at[o - 1], fsdp=at((z + o) % 8, x, core))
        for o in range(1, 8)
    ]

    passing = []
    for n, o in enumerate(ORDER):
        own = product(core * 1024 + (x + o) % 4 * 256)
        crossing[n].wait_recv()
        own = own + cross_got[n]
        if o:
            lane_sent[n] = own.astype(BF16)
            passing.append(
                send(lane_sent.at[n], lane_got.at[o - 1], xsend.at[o - 1], xrecv.at[o - 1], fsdp=at(z, (x + o) % 4, core))
            )
        else:
            block[...] = own

    for copy in around:
        copy.wait_recv()
    total = gram_z[0]
    for n in range(1, 8):
        total = total + gram_z[n]
    here = pl.ds(pl.multiple_of(core * half + eight, 8), 8)
    gram[here, :] = total
    spread = [
        send(gram.at[here], gram.at[here], g2send.at[n], g2recv.at[n], fsdp=at(z, (x + ox) % 4, core), tensor=(y + oy) % 4)
        for n, (oy, ox) in enumerate(ALONG_YX)
    ]
    for copy in spread:
        copy.wait_recv()
    away = send(gram.at[kept], gram.at[kept], g3send.at[1], g3recv.at[1], fsdp=sibling)

    for copy in passing:
        copy.wait_recv()
    block[...] = block[...] + lane_got[0].astype(F32) + lane_got[1].astype(F32) + lane_got[2].astype(F32)
    last = []
    for o in range(1, 8):
        to = (z + o) % 8
        last.append(
            send(block.at[pl.ds(pl.multiple_of(to * 32, 32), 32)], block_got.at[o - 1], zsend.at[o - 1], zrecv.at[o - 1],
                 fsdp=at(to, x, core))
        )
    away.wait_recv()
    factor_kernel(gram, inverse)
    for copy in last:
        copy.wait_recv()
    total = block[pl.ds(pl.multiple_of(z * 32, 32), 32), :]
    for n in range(7):
        total = total + block_got[n]

    def rows_of(z_of):
        return pl.ds(pl.multiple_of(core * 1024 + x * 256 + z_of * 32, 32), 32)

    here = rows_of(z)
    rounded[here, :] = dot(total, inverse[...], ((1,), (1,))).astype(BF16)
    along_z = [
        send(rounded.at[here], rounded.at[here], azsend.at[o - 1], azrecv.at[o - 1], fsdp=at((z + o) % 8, x, core))
        for o in range(1, 8)
    ]
    along_x = [[None] * 8 for _ in range(4)]

    def pass_on(zo):
        here = rows_of((z + 8 - zo) % 8)
        for o in (2, 1, 3):
            along_x[o][zo] = send(
                rounded.at[here], rounded.at[here], axsend.at[o - 1, zo], axrecv.at[o - 1, zo], fsdp=at(z, (x + o) % 4, core)
            )

    pass_on(0)
    ortho[...] = dot(panel[...], inverse[...], ((1,), (1,))).astype(BF16)
    for zo in (1, 7, 2, 6, 3, 5, 4):
        along_z[zo - 1].wait_recv()
        pass_on(zo)

    def block_of(o):
        return pl.ds(pl.multiple_of(core * 1024 + (x + 4 - o) % 4 * 256, 256), 256)

    def block_there(o):
        return pl.ds(pl.multiple_of((1 - core) * 1024 + (x + 4 - o) % 4 * 256, 256), 256)

    def feed_back(span):
        back = fast_dot(ortho[...], rounded[span, :], ((1,), (1,)))
        new_momentum[:, span] = high[:, span].astype(F32) + low[:, span].astype(F32) - 0.05 * back

    across = [send(rounded.at[block_of(0)], rounded.at[block_of(0)], acsend.at[0], acrecv.at[0], fsdp=sibling)]
    total = jnp.zeros((8, rounded.shape[1]), F32)
    part = rounded[block_of(0), :].astype(F32)
    part = part * part
    for i in range(32):
        total = total + part[8 * i : 8 * i + 8, :]
    slot = y * 4 + x
    squares[slot] = total
    spread = [
        send(squares.at[slot], squares.at[slot], sqsend.at[n], sqrecv.at[n], fsdp=at(z, (x + ox) % 4, core), tensor=(y + oy) % 4)
        for n, (oy, ox) in enumerate(ALONG_YX)
    ]
    feed_back(block_of(0))
    across[0].wait_recv()
    feed_back(block_there(0))
    for n, o in enumerate((1, 3, 2)):
        for copy in along_x[o]:
            copy.wait_recv()
        across.append(send(rounded.at[block_of(o)], rounded.at[block_of(o)], acsend.at[o], acrecv.at[o], fsdp=sibling))
        feed_back(block_of(o))
        if n < 2:
            across[-1].wait_recv()
            feed_back(block_there(o))
    for copy in spread:
        copy.wait_recv()
    total = squares[0]
    for n in range(1, 16):
        total = total + squares[n]
    halves[core] = total
    away = send(halves.at[core], halves.at[core], g3send.at[2], g3recv.at[2], fsdp=sibling)
    across[-1].wait_recv()
    feed_back(block_there(2))
    away.wait_recv()
    total = jnp.sum(halves[0] + halves[1], axis=0, keepdims=True)
    scales[...] = jnp.broadcast_to(lax.rsqrt(total + 1e-06), scales.shape)
    for copy in sent:
        copy.wait_send()


def main(grad, momentum, basis):
    rows, cols = grad.shape
    rank = basis.shape[1]
    fourth = rows // 4
    dma = pltpu.SemaphoreType.DMA
    vmem = pltpu.VMEM
    pairs = ((6,), (15,), (7,), (15,), (3,), (4,), (3,), (7,), (7,), (3, 8), (4,), (15,))
    return pl.pallas_call(
        main_kernel,
        out_shape=(
            jax.ShapeDtypeStruct((rows, cols), F32),
            jax.ShapeDtypeStruct((cols, rank), BF16),
            jax.ShapeDtypeStruct((rows, rank), BF16),
            jax.ShapeDtypeStruct((8, rank), F32),
        ),
        in_specs=[pl.BlockSpec(memory_space=pltpu.HBM)] * 3,
        out_specs=(pl.BlockSpec(memory_space=pltpu.VMEM),) * 4,
        scratch_shapes=[
            vmem((4, fourth + 8, cols), BF16),
            vmem((4, fourth + 8, cols), F32),
            vmem((cols, rank), BF16),
            vmem((rows, cols), BF16),
            vmem((rows, cols), BF16),
            vmem((cols, rows), BF16),
            vmem((cols, rows), BF16),
            vmem((4, fourth + 8, rank), F32),
            vmem((3, fourth, rank), F32),
            vmem((rows, rank), F32),
            vmem((rank, rank), F32),
            vmem((rank // 2, rank), F32),
            vmem((15, 8, rank), F32),
            vmem((8, 8, rank), F32),
            vmem((rank, rank), F32),
            vmem((rank, rank), F32),
            vmem((4, 256, rank), F32),
            vmem((4, 256, rank), F32),
            vmem((3, 256, rank), BF16),
            vmem((3, 256, rank), BF16),
            vmem((256, rank), F32),
            vmem((7, 32, rank), F32),
            vmem((16, 8, rank), F32),
            vmem((2, 8, rank), F32),
            dma((9,)),
            *[dma(shape) for shape in pairs for _ in range(2)],
        ],
        compiler_params=pltpu.CompilerParams(collective_id=0, has_side_effects=True, vmem_limit_bytes=40 << 20),
    )(*[pltpu.with_memory_space_constraint(v, pltpu.HBM) for v in (grad, momentum, basis)])


def finish_kernel(scale, momentum, rounded, ortho, scales, new_momentum, update, basis_next, part, following, sems):
    copies = [pltpu.make_async_copy(momentum, new_momentum, sems.at[0])]
    copies[0].start()
    wide = 512
    for n in range(rounded.shape[0] // wide):
        span = pl.ds(n * wide, wide)
        block = (rounded[span, :].astype(F32) * scales[:1, :]).astype(BF16)
        following[span, :] = block
        part[n] = (scale * fast_dot(ortho[...], block, ((1,), (1,)))).astype(BF16)
        copies.append(pltpu.make_async_copy(following.at[span], basis_next.at[span], sems.at[2 * n + 1]))
        copies.append(pltpu.make_async_copy(part.at[n], update.at[:, span], sems.at[2 * n + 2]))
        copies[-2].start()
        copies[-1].start()
    for copy in copies:
        copy.wait()


def finish(scale, momentum, rounded, ortho, scales):
    rows, cols = momentum.shape
    rank = ortho.shape[1]
    return pl.pallas_call(
        functools.partial(finish_kernel, scale),
        out_shape=(
            jax.ShapeDtypeStruct((rows, cols), F32),
            jax.ShapeDtypeStruct((rows, cols), BF16),
            jax.ShapeDtypeStruct((cols, rank), BF16),
        ),
        in_specs=[pl.BlockSpec(memory_space=pl.ANY)] + [pl.BlockSpec(memory_space=pltpu.VMEM)] * 3,
        out_specs=(pl.BlockSpec(memory_space=pl.ANY),) * 3,
        scratch_shapes=[
            pltpu.VMEM((cols // 512, rows, 512), BF16),
            pltpu.VMEM((cols, rank), BF16),
            pltpu.SemaphoreType.DMA((2 * cols // 512 + 1,)),
        ],
        compiler_params=pltpu.CompilerParams(vmem_limit_bytes=16 << 20),
    )(momentum, rounded, ortho, scales)


def on_device(grad, momentum, basis):
    rows_here, cols_here = grad.shape
    scale = math.sqrt(rows_here * lax.axis_size("fsdp") * cols_here * lax.axis_size("tensor") / basis.shape[1])
    momentum, rounded, ortho, scales = main(grad, momentum, basis)
    return finish(scale, momentum, rounded, ortho, scales)


def solution(mesh):
    return jax.shard_map(
        on_device,
        mesh=mesh,
        in_specs=(P("fsdp", "tensor"), P("fsdp", "tensor"), P("tensor", None)),
        out_specs=(P("fsdp", "tensor"), P("fsdp", "tensor"), P("tensor", None)),
        check_vma=False,
    )
```

```python
import functools
import math

import jax
import jax.numpy as jnp
from jax import lax
from jax.experimental import pallas as pl
from jax.experimental.pallas import tpu as pltpu
from jax.sharding import PartitionSpec as P

MESH = pl.DeviceIdType.MESH
BF16 = jnp.bfloat16
HIGH = lax.Precision.HIGHEST
F32 = jnp.float32


def dot(a, b, dims):
    return lax.dot_general(a, b, (dims, ((), ())), precision=HIGH, preferred_element_type=F32)


def inverse_factor(square):
    size = square.shape[0]
    tall = size // 8
    tiles = [square[8 * i : 8 * i + 8, :] for i in range(tall)]
    lane = lax.broadcasted_iota(jnp.int32, (8, size), 1)
    sub = lax.broadcasted_iota(jnp.int32, (8, size), 0)
    pivots = []
    for t in range(tall):
        start = 8 * t
        left = tall - t
        cols = [
            [jnp.broadcast_to(tiles[i][:, start + l : start + l + 1], (8, size)) for i in range(t, tall)]
            for l in range(8)
        ]
        mult = [[None] * left for _ in range(8)]
        group = tiles[t]
        rows = []
        pivot = jnp.zeros((8, size), F32)
        for l in range(8):
            here = cols[l][0][l : l + 1, :]
            recip = jnp.broadcast_to(1.0 / here, (8, size))
            pivot = jnp.where(sub == l, here, pivot)
            mult[l][0] = jnp.where(sub > l, cols[l][0] * recip, 0.0)
            for i in range(1, left):
                mult[l][i] = cols[l][i] * recip
            for later in range(l + 1, 8):
                across = jnp.broadcast_to(cols[later][0][l : l + 1, :], (8, size))
                for i in range(left):
                    cols[later][i] = cols[later][i] - mult[l][i] * across
            at = start + l
            row = jnp.where(lane[:1] == at, 1.0, group[l : l + 1, :])
            group = jnp.where((lane == at) & (sub > l), 0.0, group)
            group = group - mult[l][0] * jnp.broadcast_to(row, (8, size))
            row = jnp.where((lane[:1] > at) & (lane[:1] < start + 8), 0.0, row)
            rows.append(jnp.broadcast_to(row, (8, size)))
        tiles[t] = group
        pivots.append(pivot)
        for i in range(1, left):
            total = mult[0][i] * rows[0]
            for l in range(1, 8):
                total = total + mult[l][i] * rows[l]
            kept = jnp.where((lane >= start) & (lane < start + 8), 0.0, tiles[t + i])
            tiles[t + i] = kept - total
    out = []
    for i in range(tall):
        at = sub + 8 * i
        unit = jnp.where(lane == at, 1.0, jnp.where(lane < at, tiles[i], 0.0))
        out.append(unit * lax.rsqrt(pivots[i]))
    return jnp.concatenate(out, 0)


def factor_kernel(gram_ref, out_ref):
    half = gram_ref.shape[0] // 2
    first = inverse_factor(gram_ref[:half, :half])
    across = dot(first, gram_ref[:half, half:], ((1,), (0,)))
    second = inverse_factor(gram_ref[half:, half:] - dot(across, across, ((0,), (0,))))
    below = -dot(across, first, ((0,), (0,)))
    out_ref[:half, :half] = first
    out_ref[:half, half:] = jnp.zeros((half, half), F32)
    out_ref[half:, :half] = dot(second, below, ((1,), (0,)))
    out_ref[half:, half:] = second


def fast_dot(a, b, dims):
    return lax.dot_general(a, b, (dims, ((), ())), preferred_element_type=F32)


def two_parts(value):
    upper = value.astype(BF16)
    return upper, (value - upper.astype(F32)).astype(BF16)


def put(src, dst, send, recv, **where):
    copy = pltpu.make_async_remote_copy(
        src_ref=src, dst_ref=dst, send_sem=send, recv_sem=recv, device_id=where, device_id_type=MESH
    )
    copy.start()
    return copy


def place():
    flat = lax.axis_index("fsdp")
    return flat // 8, flat % 8 // 2, flat % 2, lax.axis_index("tensor")


def at(z, x, core):
    return z * 8 + x * 2 + core


def greet(others):
    barrier = pltpu.get_barrier_semaphore()
    for where in others:
        pl.semaphore_signal(barrier, inc=1, device_id=where, device_id_type=MESH)
    return lambda: pl.semaphore_wait(barrier, len(others))


ORDER = (2, 1, 3, 0)
ALONG_YX = tuple((oy, ox) for oy in range(4) for ox in range(4) if oy or ox)


def main_kernel(
    grad_hbm, momentum_hbm, basis_hbm,
    new_momentum, rounded, ortho, ortho_low, scales,
    grad_in, momentum_in, basis_in, high, low, high_turned, low_turned, piece, piece_sent, panel_got, panel, panel_own, panel_there,
    gram_own, gram_half, gram_got, gram_z, gram, inverse,
    cross, cross_got, lane_sent, lane_got, block, block_got, squares, squares_z, halves,
    load_sem, ysend, yrecv, gsend, grecv, zgsend, zgrecv, g2send, g2recv, g3send, g3recv,
    csend, crecv, xsend, xrecv, zsend, zrecv, azsend, azrecv, axsend, axrecv, acsend, acrecv, sqsend, sqrecv, sqzsend, sqzrecv,
):
    z, x, core, y = place()
    rows = grad_hbm.shape[0]
    fourth = rows // 4
    taller = fourth + 8
    sibling = at(z, x, 1 - core)
    others = [{"fsdp": at((z + o) % 8, x, core)} for o in range(1, 8)]
    others += [{"fsdp": at(z, (x + ox) % 4, core), "tensor": (y + oy) % 4} for oy, ox in ALONG_YX]
    others += [{"fsdp": sibling}]
    greeted = greet(others)
    basis_load = pltpu.make_async_copy(basis_hbm, basis_in, load_sem.at[8])
    basis_load.start()
    loads = []
    for n, o in enumerate(ORDER):
        p = (y + o) % 4
        start = pl.multiple_of(p * fourth - 8 * (p % 2), 16)
        for which, (src, dst) in enumerate(((grad_hbm, grad_in), (momentum_hbm, momentum_in))):
            load = pltpu.make_async_copy(src.at[pl.ds(start, taller)], dst.at[n], load_sem.at[2 * n + which])
            load.start()
            loads.append(load)
    basis_load.wait()
    sent = []

    def send(src, dst, send_sem, recv_sem, **where):
        copy = put(src, dst, send_sem, recv_sem, **where)
        sent.append(copy)
        return copy

    copies = []
    for n, o in enumerate(ORDER):
        p = (y + o) % 4
        start = pl.multiple_of(p * fourth - 8 * (p % 2), 16)
        skip = pl.multiple_of(8 * (p % 2), 8)
        loads[2 * n].wait()
        loads[2 * n + 1].wait()
        upper, lower = two_parts(momentum_in[n] + grad_in[n].astype(F32))
        high[pl.ds(start, taller), :] = upper
        low[pl.ds(start, taller), :] = lower
        basis_v = basis_in[...]
        piece[n] = fast_dot(upper, basis_v, ((1,), (0,))) + fast_dot(lower, basis_v, ((1,), (0,)))
        if n == 0:
            greeted()
        if o:
            piece_sent[n] = piece[n, pl.ds(skip, fourth), :].astype(BF16)
            copies.append(send(piece_sent.at[n], panel_got.at[o - 1], ysend.at[o - 1], yrecv.at[o - 1], tensor=p))
    for n in range(8):
        wide = slice(256 * n, 256 * n + 256)
        high_turned[wide, :] = high[:, wide].T
        low_turned[wide, :] = low[:, wide].T
    skip = pl.multiple_of(8 * (y % 2), 8)
    total = piece[3, pl.ds(skip, fourth), :]
    for copy in copies:
        copy.wait_recv()
    for o in (1, 2, 3):
        total = total + panel_got[o - 1].astype(F32)
    mine = pl.ds(pl.multiple_of(y * fourth, 8), fourth)
    panel_own[...] = total.astype(BF16)
    gathers = [
        send(panel_own, panel_there.at[o - 1], ysend.at[2 + o], yrecv.at[2 + o], tensor=(y + o) % 4) for o in (1, 2, 3)
    ]

    half = 128
    total = panel_own[...].astype(F32)
    panel[mine, :] = total
    gram_own[...] = fast_dot(panel_own[...], panel_own[...], ((0,), (0,)))
    away = send(gram_own.at[pl.ds(pl.multiple_of((1 - core) * half, half), half)], gram_half, g3send.at[0], g3recv.at[0], fsdp=sibling)
    away.wait_recv()
    kept = pl.ds(pl.multiple_of(core * half, half), half)
    gram_half[...] = gram_half[...] + gram_own[kept, :]
    spread = []
    for n, (oy, ox) in enumerate(ALONG_YX):
        ty, tx = (y + oy) % 4, (x + ox) % 4
        src = gram_half.at[pl.ds(pl.multiple_of((ty * 4 + tx) * 8, 8), 8)]
        spread.append(send(src, gram_got.at[n], gsend.at[n], grecv.at[n], fsdp=at(z, tx, core), tensor=ty))
    for copy in gathers:
        copy.wait_recv()
    for o in (1, 2, 3):
        panel[pl.ds(pl.multiple_of((y + 4 - o) % 4 * fourth, 8), fourth), :] = panel_there[o - 1].astype(F32)
    panel_high = panel[...].astype(BF16)

    def product(start):
        upper = high_turned[pl.ds(pl.multiple_of(start, 256), 256), :]
        lower = low_turned[pl.ds(pl.multiple_of(start, 256), 256), :]
        return (
            fast_dot(upper, panel_high, ((1,), (0,)))
            + fast_dot(lower, panel_high, ((1,), (0,)))
        )

    crossing = []
    for n, o in enumerate(ORDER):
        cross[n] = product((1 - core) * 1024 + (x + o) % 4 * 256)
        crossing.append(send(cross.at[n], cross_got.at[n], csend.at[n], crecv.at[n], fsdp=sibling))
    for copy in spread:
        copy.wait_recv()
    eight = (y * 4 + x) * 8
    total = gram_half[pl.ds(pl.multiple_of(eight, 8), 8), :]
    for n in range(15):
        total = total + gram_got[n]
    gram_z[z] = total
    around = [
        send(gram_z.at[z], gram_z.at[z], zgsend.at[o - 1], zgrecv.at[o - 1], fsdp=at((z + o) % 8, x, core))
        for o in range(1, 8)
    ]

    passing = []
    for n, o in enumerate(ORDER):
        own = product(core * 1024 + (x + o) % 4 * 256)
        crossing[n].wait_recv()
        own = own + cross_got[n]
        if o:
            lane_sent[n] = own.astype(BF16)
            passing.append(
                send(lane_sent.at[n], lane_got.at[o - 1], xsend.at[o - 1], xrecv.at[o - 1], fsdp=at(z, (x + o) % 4, core))
            )
        else:
            block[...] = own

    for copy in around:
        copy.wait_recv()
    total = gram_z[0]
    for n in range(1, 8):
        total = total + gram_z[n]
    here = pl.ds(pl.multiple_of(core * half + eight, 8), 8)
    gram[here, :] = total
    spread = [
        send(gram.at[here], gram.at[here], g2send.at[n], g2recv.at[n], fsdp=at(z, (x + ox) % 4, core), tensor=(y + oy) % 4)
        for n, (oy, ox) in enumerate(ALONG_YX)
    ]
    for copy in spread:
        copy.wait_recv()
    away = send(gram.at[kept], gram.at[kept], g3send.at[1], g3recv.at[1], fsdp=sibling)

    for copy in passing:
        copy.wait_recv()
    block[...] = block[...] + lane_got[0].astype(F32) + lane_got[1].astype(F32) + lane_got[2].astype(F32)
    last = []
    for o in range(1, 8):
        to = (z + o) % 8
        last.append(
            send(block.at[pl.ds(pl.multiple_of(to * 32, 32), 32)], block_got.at[o - 1], zsend.at[o - 1], zrecv.at[o - 1],
                 fsdp=at(to, x, core))
        )
    away.wait_recv()
    factor_kernel(gram, inverse)
    for copy in last:
        copy.wait_recv()
    total = block[pl.ds(pl.multiple_of(z * 32, 32), 32), :]
    for n in range(7):
        total = total + block_got[n]

    def rows_of(z_of):
        return pl.ds(pl.multiple_of(core * 1024 + x * 256 + z_of * 32, 32), 32)

    here = rows_of(z)
    own = dot(total, inverse[...], ((1,), (1,))).astype(BF16)
    rounded[here, :] = own
    along_z = [
        send(rounded.at[here], rounded.at[here], azsend.at[o - 1], azrecv.at[o - 1], fsdp=at((z + o) % 8, x, core))
        for o in range(1, 8)
    ]
    along_x = [[None] * 8 for _ in range(4)]

    def pass_on(zo):
        here = rows_of((z + 8 - zo) % 8)
        for o in (2, 1, 3):
            along_x[o][zo] = send(
                rounded.at[here], rounded.at[here], axsend.at[o - 1, zo], axrecv.at[o - 1, zo], fsdp=at(z, (x + o) % 4, core)
            )

    pass_on(0)
    own = own.astype(F32)
    slot = y * 4 + x
    squares[slot] = jnp.sum(own * own, axis=0, keepdims=True)
    spread = [
        send(squares.at[slot], squares.at[slot], sqsend.at[n], sqrecv.at[n], fsdp=at(z, (x + ox) % 4, core), tensor=(y + oy) % 4)
        for n, (oy, ox) in enumerate(ALONG_YX)
    ]
    upper, lower = two_parts(dot(panel[...], inverse[...], ((1,), (1,))))
    ortho[...] = upper
    ortho_low[...] = lower
    for zo in (1, 7, 2, 6, 3, 5):
        along_z[zo - 1].wait_recv()
        pass_on(zo)
    for copy in spread:
        copy.wait_recv()
    total = squares[0]
    for n in range(1, 16):
        total = total + squares[n]
    squares_z[z] = total
    around = [
        send(squares_z.at[z], squares_z.at[z], sqzsend.at[o - 1], sqzrecv.at[o - 1], fsdp=at((z + o) % 8, x, core))
        for o in range(1, 8)
    ]
    along_z[3].wait_recv()
    pass_on(4)

    def block_of(o):
        return pl.ds(pl.multiple_of(core * 1024 + (x + 4 - o) % 4 * 256, 256), 256)

    def block_there(o):
        return pl.ds(pl.multiple_of((1 - core) * 1024 + (x + 4 - o) % 4 * 256, 256), 256)

    def feed_back(span):
        back = fast_dot(ortho[...], rounded[span, :], ((1,), (1,)))
        new_momentum[:, span] = high[:, span].astype(F32) + low[:, span].astype(F32) - 0.05 * back

    across = [send(rounded.at[block_of(0)], rounded.at[block_of(0)], acsend.at[0], acrecv.at[0], fsdp=sibling)]
    feed_back(block_of(0))
    across[0].wait_recv()
    feed_back(block_there(0))
    for n, o in enumerate((1, 3, 2)):
        for copy in along_x[o]:
            copy.wait_recv()
        across.append(send(rounded.at[block_of(o)], rounded.at[block_of(o)], acsend.at[o], acrecv.at[o], fsdp=sibling))
        feed_back(block_of(o))
        if n < 2:
            across[-1].wait_recv()
            feed_back(block_there(o))
    for copy in around:
        copy.wait_recv()
    total = squares_z[0]
    for n in range(1, 8):
        total = total + squares_z[n]
    halves[core] = total
    away = send(halves.at[core], halves.at[core], g3send.at[2], g3recv.at[2], fsdp=sibling)
    across[-1].wait_recv()
    feed_back(block_there(2))
    away.wait_recv()
    total = halves[0] + halves[1]
    scales[...] = jnp.broadcast_to(lax.rsqrt(total + 1e-06), scales.shape)
    for copy in sent:
        copy.wait_send()


def main(grad, momentum, basis):
    rows, cols = grad.shape
    rank = basis.shape[1]
    fourth = rows // 4
    dma = pltpu.SemaphoreType.DMA
    vmem = pltpu.VMEM
    pairs = ((6,), (15,), (7,), (15,), (3,), (4,), (3,), (7,), (7,), (3, 8), (4,), (15,), (7,))
    return pl.pallas_call(
        main_kernel,
        out_shape=(
            jax.ShapeDtypeStruct((rows, cols), F32),
            jax.ShapeDtypeStruct((cols, rank), BF16),
            jax.ShapeDtypeStruct((rows, rank), BF16),
            jax.ShapeDtypeStruct((rows, rank), BF16),
            jax.ShapeDtypeStruct((8, rank), F32),
        ),
        in_specs=[pl.BlockSpec(memory_space=pltpu.HBM)] * 3,
        out_specs=(pl.BlockSpec(memory_space=pltpu.VMEM),) * 5,
        scratch_shapes=[
            vmem((4, fourth + 8, cols), BF16),
            vmem((4, fourth + 8, cols), F32),
            vmem((cols, rank), BF16),
            vmem((rows, cols), BF16),
            vmem((rows, cols), BF16),
            vmem((cols, rows), BF16),
            vmem((cols, rows), BF16),
            vmem((4, fourth + 8, rank), F32),
            vmem((3, fourth, rank), BF16),
            vmem((3, fourth, rank), BF16),
            vmem((rows, rank), F32),
            vmem((fourth, rank), BF16),
            vmem((3, fourth, rank), BF16),
            vmem((rank, rank), F32),
            vmem((rank // 2, rank), F32),
            vmem((15, 8, rank), F32),
            vmem((8, 8, rank), F32),
            vmem((rank, rank), F32),
            vmem((rank, rank), F32),
            vmem((4, 256, rank), F32),
            vmem((4, 256, rank), F32),
            vmem((3, 256, rank), BF16),
            vmem((3, 256, rank), BF16),
            vmem((256, rank), F32),
            vmem((7, 32, rank), F32),
            vmem((16, 1, rank), F32),
            vmem((8, 1, rank), F32),
            vmem((2, 1, rank), F32),
            dma((9,)),
            *[dma(shape) for shape in pairs for _ in range(2)],
        ],
        compiler_params=pltpu.CompilerParams(collective_id=0, has_side_effects=True, vmem_limit_bytes=40 << 20),
    )(*[pltpu.with_memory_space_constraint(v, pltpu.HBM) for v in (grad, momentum, basis)])


def finish_kernel(scale, momentum, rounded, ortho, ortho_low, scales, new_momentum, update, basis_next, part, following, sems):
    copies = [pltpu.make_async_copy(momentum, new_momentum, sems.at[0])]
    copies[0].start()
    wide = 512
    for n in range(rounded.shape[0] // wide):
        span = pl.ds(n * wide, wide)
        block = (rounded[span, :].astype(F32) * scales[:1, :]).astype(BF16)
        following[span, :] = block
        step = fast_dot(ortho[...], block, ((1,), (1,))) + fast_dot(ortho_low[...], block, ((1,), (1,)))
        part[n] = (scale * step).astype(BF16)
        copies.append(pltpu.make_async_copy(following.at[span], basis_next.at[span], sems.at[2 * n + 1]))
        copies.append(pltpu.make_async_copy(part.at[n], update.at[:, span], sems.at[2 * n + 2]))
        copies[-2].start()
        copies[-1].start()
    for copy in copies:
        copy.wait()


def finish(scale, momentum, rounded, ortho, ortho_low, scales):
    rows, cols = momentum.shape
    rank = ortho.shape[1]
    return pl.pallas_call(
        functools.partial(finish_kernel, scale),
        out_shape=(
            jax.ShapeDtypeStruct((rows, cols), F32),
            jax.ShapeDtypeStruct((rows, cols), BF16),
            jax.ShapeDtypeStruct((cols, rank), BF16),
        ),
        in_specs=[pl.BlockSpec(memory_space=pl.ANY)] + [pl.BlockSpec(memory_space=pltpu.VMEM)] * 4,
        out_specs=(pl.BlockSpec(memory_space=pl.ANY),) * 3,
        scratch_shapes=[
            pltpu.VMEM((cols // 512, rows, 512), BF16),
            pltpu.VMEM((cols, rank), BF16),
            pltpu.SemaphoreType.DMA((2 * cols // 512 + 1,)),
        ],
        compiler_params=pltpu.CompilerParams(vmem_limit_bytes=16 << 20),
    )(momentum, rounded, ortho, ortho_low, scales)


def on_device(grad, momentum, basis):
    rows_here, cols_here = grad.shape
    scale = math.sqrt(rows_here * lax.axis_size("fsdp") * cols_here * lax.axis_size("tensor") / basis.shape[1])
    momentum, *rest = main(grad, momentum, basis)
    return finish(scale, momentum, *rest)


def solution(mesh):
    return jax.shard_map(
        on_device,
        mesh=mesh,
        in_specs=(P("fsdp", "tensor"), P("fsdp", "tensor"), P("tensor", None)),
        out_specs=(P("fsdp", "tensor"), P("fsdp", "tensor"), P("tensor", None)),
        check_vma=False,
    )
```

```python
import functools
import math

import jax
import jax.numpy as jnp
from jax import lax
from jax.experimental import pallas as pl
from jax.experimental.pallas import tpu as pltpu
from jax.sharding import PartitionSpec as P

MESH = pl.DeviceIdType.MESH
BF16 = jnp.bfloat16
HIGH = lax.Precision.HIGHEST
F32 = jnp.float32


def dot(a, b, dims):
    return lax.dot_general(a, b, (dims, ((), ())), precision=HIGH, preferred_element_type=F32)


def inverse_factor(square):
    size = square.shape[0]
    tall = size // 8
    tiles = [square[8 * i : 8 * i + 8, :] for i in range(tall)]
    lane = lax.broadcasted_iota(jnp.int32, (8, size), 1)
    sub = lax.broadcasted_iota(jnp.int32, (8, size), 0)
    pivots = []
    for t in range(tall):
        start = 8 * t
        left = tall - t
        cols = [
            [jnp.broadcast_to(tiles[i][:, start + l : start + l + 1], (8, size)) for i in range(t, tall)]
            for l in range(8)
        ]
        mult = [[None] * left for _ in range(8)]
        group = tiles[t]
        rows = []
        pivot = jnp.zeros((8, size), F32)
        for l in range(8):
            here = cols[l][0][l : l + 1, :]
            recip = jnp.broadcast_to(1.0 / here, (8, size))
            pivot = jnp.where(sub == l, here, pivot)
            mult[l][0] = jnp.where(sub > l, cols[l][0] * recip, 0.0)
            for i in range(1, left):
                mult[l][i] = cols[l][i] * recip
            for later in range(l + 1, 8):
                across = jnp.broadcast_to(cols[later][0][l : l + 1, :], (8, size))
                for i in range(left):
                    cols[later][i] = cols[later][i] - mult[l][i] * across
            at = start + l
            row = jnp.where(lane[:1] == at, 1.0, group[l : l + 1, :])
            group = jnp.where((lane == at) & (sub > l), 0.0, group)
            group = group - mult[l][0] * jnp.broadcast_to(row, (8, size))
            row = jnp.where((lane[:1] > at) & (lane[:1] < start + 8), 0.0, row)
            rows.append(jnp.broadcast_to(row, (8, size)))
        tiles[t] = group
        pivots.append(pivot)
        for i in range(1, left):
            total = mult[0][i] * rows[0]
            for l in range(1, 8):
                total = total + mult[l][i] * rows[l]
            kept = jnp.where((lane >= start) & (lane < start + 8), 0.0, tiles[t + i])
            tiles[t + i] = kept - total
    out = []
    for i in range(tall):
        at = sub + 8 * i
        unit = jnp.where(lane == at, 1.0, jnp.where(lane < at, tiles[i], 0.0))
        out.append(unit * lax.rsqrt(pivots[i]))
    return jnp.concatenate(out, 0)


def factor_kernel(gram_ref, out_ref):
    half = gram_ref.shape[0] // 2
    first = inverse_factor(gram_ref[:half, :half])
    across = dot(first, gram_ref[:half, half:], ((1,), (0,)))
    second = inverse_factor(gram_ref[half:, half:] - dot(across, across, ((0,), (0,))))
    below = -dot(across, first, ((0,), (0,)))
    out_ref[:half, :half] = first
    out_ref[:half, half:] = jnp.zeros((half, half), F32)
    out_ref[half:, :half] = dot(second, below, ((1,), (0,)))
    out_ref[half:, half:] = second


def fast_dot(a, b, dims):
    return lax.dot_general(a, b, (dims, ((), ())), preferred_element_type=F32)


def two_parts(value):
    upper = value.astype(BF16)
    return upper, (value - upper.astype(F32)).astype(BF16)


def put(src, dst, send, recv, **where):
    copy = pltpu.make_async_remote_copy(
        src_ref=src, dst_ref=dst, send_sem=send, recv_sem=recv, device_id=where, device_id_type=MESH
    )
    copy.start()
    return copy


def place():
    flat = lax.axis_index("fsdp")
    return flat // 8, flat % 8 // 2, flat % 2, lax.axis_index("tensor")


def at(z, x, core):
    return z * 8 + x * 2 + core


def greet(others):
    barrier = pltpu.get_barrier_semaphore()
    for where in others:
        pl.semaphore_signal(barrier, inc=1, device_id=where, device_id_type=MESH)
    return lambda: pl.semaphore_wait(barrier, len(others))


ORDER = (2, 1, 3, 0)
ALONG_YX = tuple(
    sorted(
        ((oy, ox) for oy in range(4) for ox in range(4) if oy or ox),
        key=lambda o: -min(o[0], 4 - o[0]) - min(o[1], 4 - o[1]),
    )
)
ALONG_Z = (4, 3, 5, 2, 6, 1, 7)


def main_kernel(
    grad_hbm, momentum_hbm, basis_hbm,
    new_momentum, rounded, ortho, ortho_low, scales,
    grad_in, momentum_in, basis_in, high, low, high_turned, low_turned, piece, piece_sent, panel_got, panel, panel_own, panel_there,
    gram_own, gram_half, gram_got, gram_z, gram, inverse,
    cross, cross_got, lane_sent, lane_got, block, block_got, squares, squares_z, halves,
    load_sem, ysend, yrecv, gsend, grecv, zgsend, zgrecv, g2send, g2recv, g3send, g3recv,
    csend, crecv, xsend, xrecv, zsend, zrecv, azsend, azrecv, axsend, axrecv, acsend, acrecv, sqsend, sqrecv, sqzsend, sqzrecv,
):
    z, x, core, y = place()
    rows = grad_hbm.shape[0]
    fourth = rows // 4
    taller = fourth + 8
    sibling = at(z, x, 1 - core)
    across_z = [{"fsdp": at((z + o) % 8, x, core)} for o in ALONG_Z]
    others = across_z + [{"tensor": (y + o) % 4} for o in (2, 1, 3)]
    others += [{"fsdp": at(z, (x + o) % 4, core)} for o in (2, 1, 3)]
    others += [{"fsdp": sibling}]
    greeted = greet(others)
    basis_load = pltpu.make_async_copy(basis_hbm, basis_in, load_sem.at[8])
    basis_load.start()
    loads = []
    for n, o in enumerate(ORDER):
        p = (y + o) % 4
        start = pl.multiple_of(p * fourth - 8 * (p % 2), 16)
        for which, (src, dst) in enumerate(((grad_hbm, grad_in), (momentum_hbm, momentum_in))):
            load = pltpu.make_async_copy(src.at[pl.ds(start, taller)], dst.at[n], load_sem.at[2 * n + which])
            load.start()
            loads.append(load)
    basis_load.wait()
    sent = []

    def send(src, dst, send_sem, recv_sem, **where):
        copy = put(src, dst, send_sem, recv_sem, **where)
        sent.append(copy)
        return copy

    copies = []
    for n, o in enumerate(ORDER):
        p = (y + o) % 4
        start = pl.multiple_of(p * fourth - 8 * (p % 2), 16)
        skip = pl.multiple_of(8 * (p % 2), 8)
        loads[2 * n].wait()
        loads[2 * n + 1].wait()
        upper, lower = two_parts(momentum_in[n] + grad_in[n].astype(F32))
        high[pl.ds(start, taller), :] = upper
        low[pl.ds(start, taller), :] = lower
        basis_v = basis_in[...]
        piece[n] = fast_dot(upper, basis_v, ((1,), (0,))) + fast_dot(lower, basis_v, ((1,), (0,)))
        if n == 0:
            greeted()
        if o:
            piece_sent[n] = piece[n, pl.ds(skip, fourth), :].astype(BF16)
            copies.append(send(piece_sent.at[n], panel_got.at[o - 1], ysend.at[o - 1], yrecv.at[o - 1], tensor=p))
    for n in range(8):
        wide = slice(256 * n, 256 * n + 256)
        high_turned[wide, :] = high[:, wide].T
        low_turned[wide, :] = low[:, wide].T
    skip = pl.multiple_of(8 * (y % 2), 8)
    total = piece[3, pl.ds(skip, fourth), :]
    for copy in copies:
        copy.wait_recv()
    for o in (1, 2, 3):
        total = total + panel_got[o - 1].astype(F32)
    mine = pl.ds(pl.multiple_of(y * fourth, 8), fourth)
    panel_own[...] = total.astype(BF16)
    gathers = [
        send(panel_own, panel_there.at[o - 1], ysend.at[2 + o], yrecv.at[2 + o], tensor=(y + o) % 4) for o in (1, 2, 3)
    ]

    half = 128
    total = panel_own[...].astype(F32)
    panel[mine, :] = total
    gram_own[...] = fast_dot(panel_own[...], panel_own[...], ((0,), (0,)))
    away = send(gram_own.at[pl.ds(pl.multiple_of((1 - core) * half, half), half)], gram_half, g3send.at[0], g3recv.at[0], fsdp=sibling)
    away.wait_recv()
    kept = pl.ds(pl.multiple_of(core * half, half), half)
    gram_half[...] = gram_half[...] + gram_own[kept, :]
    spread = []
    for n, (oy, ox) in enumerate(ALONG_YX):
        ty, tx = (y + oy) % 4, (x + ox) % 4
        src = gram_half.at[pl.ds(pl.multiple_of((ty * 4 + tx) * 8, 8), 8)]
        spread.append(send(src, gram_got.at[n], gsend.at[n], grecv.at[n], fsdp=at(z, tx, core), tensor=ty))
    for copy in gathers:
        copy.wait_recv()
    for o in (1, 2, 3):
        panel[pl.ds(pl.multiple_of((y + 4 - o) % 4 * fourth, 8), fourth), :] = panel_there[o - 1].astype(F32)
    panel_high = panel[...].astype(BF16)

    def product(start):
        upper = high_turned[pl.ds(pl.multiple_of(start, 256), 256), :]
        lower = low_turned[pl.ds(pl.multiple_of(start, 256), 256), :]
        return (
            fast_dot(upper, panel_high, ((1,), (0,)))
            + fast_dot(lower, panel_high, ((1,), (0,)))
        )

    crossing = []
    for n, o in enumerate(ORDER):
        cross[n] = product((1 - core) * 1024 + (x + o) % 4 * 256)
        crossing.append(send(cross.at[n], cross_got.at[n], csend.at[n], crecv.at[n], fsdp=sibling))
    passing = []
    for n, o in ((0, 2), (1, 1)):
        own = product(core * 1024 + (x + o) % 4 * 256)
        crossing[n].wait_recv()
        own = own + cross_got[n]
        if o:
            lane_sent[n] = own.astype(BF16)
            passing.append(
                send(lane_sent.at[n], lane_got.at[o - 1], xsend.at[o - 1], xrecv.at[o - 1], fsdp=at(z, (x + o) % 4, core))
            )
        else:
            block[...] = own
    for copy in spread:
        copy.wait_recv()
    eight = (y * 4 + x) * 8
    total = gram_half[pl.ds(pl.multiple_of(eight, 8), 8), :]
    for n in range(15):
        total = total + gram_got[n]
    gram_z[z] = total
    around = [
        send(gram_z.at[z], gram_z.at[z], zgsend.at[o - 1], zgrecv.at[o - 1], fsdp=at((z + o) % 8, x, core))
        for o in ALONG_Z
    ]
    for n, o in ((2, 3), (3, 0)):
        own = product(core * 1024 + (x + o) % 4 * 256)
        crossing[n].wait_recv()
        own = own + cross_got[n]
        if o:
            lane_sent[n] = own.astype(BF16)
            passing.append(
                send(lane_sent.at[n], lane_got.at[o - 1], xsend.at[o - 1], xrecv.at[o - 1], fsdp=at(z, (x + o) % 4, core))
            )
        else:
            block[...] = own

    for copy in around:
        copy.wait_recv()
    total = gram_z[0]
    for n in range(1, 8):
        total = total + gram_z[n]
    here = pl.ds(pl.multiple_of(core * half + eight, 8), 8)
    gram[here, :] = total
    spread = [
        send(gram.at[here], gram.at[here], g2send.at[n], g2recv.at[n], fsdp=at(z, (x + ox) % 4, core), tensor=(y + oy) % 4)
        for n, (oy, ox) in enumerate(ALONG_YX)
    ]
    for copy in spread:
        copy.wait_recv()
    away = send(gram.at[kept], gram.at[kept], g3send.at[1], g3recv.at[1], fsdp=sibling)

    for copy in passing:
        copy.wait_recv()
    block[...] = block[...] + lane_got[0].astype(F32) + lane_got[1].astype(F32) + lane_got[2].astype(F32)
    last = []
    for o in ALONG_Z:
        to = (z + o) % 8
        last.append(
            send(block.at[pl.ds(pl.multiple_of(to * 32, 32), 32)], block_got.at[o - 1], zsend.at[o - 1], zrecv.at[o - 1],
                 fsdp=at(to, x, core))
        )
    away.wait_recv()
    factor_kernel(gram, inverse)
    for copy in last:
        copy.wait_recv()
    total = block[pl.ds(pl.multiple_of(z * 32, 32), 32), :]
    for n in range(7):
        total = total + block_got[n]

    def rows_of(z_of):
        return pl.ds(pl.multiple_of(core * 1024 + x * 256 + z_of * 32, 32), 32)

    here = rows_of(z)
    own = dot(total, inverse[...], ((1,), (1,))).astype(BF16)
    rounded[here, :] = own
    along_z = [
        send(rounded.at[here], rounded.at[here], azsend.at[o - 1], azrecv.at[o - 1], fsdp=at((z + o) % 8, x, core))
        for o in range(1, 8)
    ]
    along_x = [[None] * 8 for _ in range(4)]

    def pass_on(zo):
        here = rows_of((z + 8 - zo) % 8)
        for o in (2, 1, 3):
            along_x[o][zo] = send(
                rounded.at[here], rounded.at[here], axsend.at[o - 1, zo], axrecv.at[o - 1, zo], fsdp=at(z, (x + o) % 4, core)
            )

    pass_on(0)
    own = own.astype(F32)
    slot = y * 4 + x
    squares[slot] = jnp.sum(own * own, axis=0, keepdims=True)
    spread = [
        send(squares.at[slot], squares.at[slot], sqsend.at[n], sqrecv.at[n], fsdp=at(z, (x + ox) % 4, core), tensor=(y + oy) % 4)
        for n, (oy, ox) in enumerate(ALONG_YX)
    ]
    upper, lower = two_parts(dot(panel[...], inverse[...], ((1,), (1,))))
    ortho[...] = upper
    ortho_low[...] = lower
    for zo in (1, 7, 2, 6, 3, 5):
        along_z[zo - 1].wait_recv()
        pass_on(zo)
    for copy in spread:
        copy.wait_recv()
    total = squares[0]
    for n in range(1, 16):
        total = total + squares[n]
    squares_z[z] = total
    around = [
        send(squares_z.at[z], squares_z.at[z], sqzsend.at[o - 1], sqzrecv.at[o - 1], fsdp=at((z + o) % 8, x, core))
        for o in ALONG_Z
    ]
    along_z[3].wait_recv()
    pass_on(4)

    def block_of(o):
        return pl.ds(pl.multiple_of(core * 1024 + (x + 4 - o) % 4 * 256, 256), 256)

    def block_there(o):
        return pl.ds(pl.multiple_of((1 - core) * 1024 + (x + 4 - o) % 4 * 256, 256), 256)

    def feed_back(span):
        back = fast_dot(ortho[...], rounded[span, :], ((1,), (1,)))
        new_momentum[:, span] = high[:, span].astype(F32) + low[:, span].astype(F32) - 0.05 * back

    across = [send(rounded.at[block_of(0)], rounded.at[block_of(0)], acsend.at[0], acrecv.at[0], fsdp=sibling)]
    feed_back(block_of(0))
    across[0].wait_recv()
    feed_back(block_there(0))
    for n, o in enumerate((1, 3, 2)):
        for copy in along_x[o]:
            copy.wait_recv()
        across.append(send(rounded.at[block_of(o)], rounded.at[block_of(o)], acsend.at[o], acrecv.at[o], fsdp=sibling))
        feed_back(block_of(o))
        if n < 2:
            across[-1].wait_recv()
            feed_back(block_there(o))
    for copy in around:
        copy.wait_recv()
    total = squares_z[0]
    for n in range(1, 8):
        total = total + squares_z[n]
    halves[core] = total
    away = send(halves.at[core], halves.at[core], g3send.at[2], g3recv.at[2], fsdp=sibling)
    across[-1].wait_recv()
    feed_back(block_there(2))
    away.wait_recv()
    total = halves[0] + halves[1]
    scales[...] = jnp.broadcast_to(lax.rsqrt(total + 1e-06), scales.shape)
    for copy in sent:
        copy.wait_send()


def main(grad, momentum, basis):
    rows, cols = grad.shape
    rank = basis.shape[1]
    fourth = rows // 4
    dma = pltpu.SemaphoreType.DMA
    vmem = pltpu.VMEM
    pairs = ((6,), (15,), (7,), (15,), (3,), (4,), (3,), (7,), (7,), (3, 8), (4,), (15,), (7,))
    return pl.pallas_call(
        main_kernel,
        out_shape=(
            jax.ShapeDtypeStruct((rows, cols), F32),
            jax.ShapeDtypeStruct((cols, rank), BF16),
            jax.ShapeDtypeStruct((rows, rank), BF16),
            jax.ShapeDtypeStruct((rows, rank), BF16),
            jax.ShapeDtypeStruct((8, rank), F32),
        ),
        in_specs=[pl.BlockSpec(memory_space=pltpu.HBM)] * 3,
        out_specs=(pl.BlockSpec(memory_space=pltpu.VMEM),) * 5,
        scratch_shapes=[
            vmem((4, fourth + 8, cols), BF16),
            vmem((4, fourth + 8, cols), F32),
            vmem((cols, rank), BF16),
            vmem((rows, cols), BF16),
            vmem((rows, cols), BF16),
            vmem((cols, rows), BF16),
            vmem((cols, rows), BF16),
            vmem((4, fourth + 8, rank), F32),
            vmem((3, fourth, rank), BF16),
            vmem((3, fourth, rank), BF16),
            vmem((rows, rank), F32),
            vmem((fourth, rank), BF16),
            vmem((3, fourth, rank), BF16),
            vmem((rank, rank), F32),
            vmem((rank // 2, rank), F32),
            vmem((15, 8, rank), F32),
            vmem((8, 8, rank), F32),
            vmem((rank, rank), F32),
            vmem((rank, rank), F32),
            vmem((4, 256, rank), F32),
            vmem((4, 256, rank), F32),
            vmem((3, 256, rank), BF16),
            vmem((3, 256, rank), BF16),
            vmem((256, rank), F32),
            vmem((7, 32, rank), F32),
            vmem((16, 1, rank), F32),
            vmem((8, 1, rank), F32),
            vmem((2, 1, rank), F32),
            dma((9,)),
            *[dma(shape) for shape in pairs for _ in range(2)],
        ],
        compiler_params=pltpu.CompilerParams(collective_id=0, has_side_effects=True, vmem_limit_bytes=40 << 20),
    )(*[pltpu.with_memory_space_constraint(v, pltpu.HBM) for v in (grad, momentum, basis)])


def finish_kernel(scale, momentum, rounded, ortho, ortho_low, scales, new_momentum, update, basis_next, part, following, sems):
    wide = 512
    many = rounded.shape[0] // wide
    tall = momentum.shape[0] // many
    copies = []
    for n in range(many):
        span = pl.ds(n * tall, tall)
        copies.append(pltpu.make_async_copy(momentum.at[span], new_momentum.at[span], sems.at[2 * many + n]))
        copies[-1].start()
    for n in range(many):
        span = pl.ds(n * wide, wide)
        block = (rounded[span, :].astype(F32) * scales[:1, :]).astype(BF16)
        following[span, :] = block
        step = fast_dot(ortho[...], block, ((1,), (1,))) + fast_dot(ortho_low[...], block, ((1,), (1,)))
        part[n] = (scale * step).astype(BF16)
        copies.append(pltpu.make_async_copy(following.at[span], basis_next.at[span], sems.at[2 * n]))
        copies.append(pltpu.make_async_copy(part.at[n], update.at[:, span], sems.at[2 * n + 1]))
        copies[-2].start()
        copies[-1].start()
    for copy in copies:
        copy.wait()


def finish(scale, momentum, rounded, ortho, ortho_low, scales):
    rows, cols = momentum.shape
    rank = ortho.shape[1]
    return pl.pallas_call(
        functools.partial(finish_kernel, scale),
        out_shape=(
            jax.ShapeDtypeStruct((rows, cols), F32),
            jax.ShapeDtypeStruct((rows, cols), BF16),
            jax.ShapeDtypeStruct((cols, rank), BF16),
        ),
        in_specs=[pl.BlockSpec(memory_space=pl.ANY)] + [pl.BlockSpec(memory_space=pltpu.VMEM)] * 4,
        out_specs=(pl.BlockSpec(memory_space=pl.ANY),) * 3,
        scratch_shapes=[
            pltpu.VMEM((cols // 512, rows, 512), BF16),
            pltpu.VMEM((cols, rank), BF16),
            pltpu.SemaphoreType.DMA((3 * cols // 512,)),
        ],
        compiler_params=pltpu.CompilerParams(vmem_limit_bytes=16 << 20),
    )(momentum, rounded, ortho, ortho_low, scales)


def on_device(grad, momentum, basis):
    rows_here, cols_here = grad.shape
    scale = math.sqrt(rows_here * lax.axis_size("fsdp") * cols_here * lax.axis_size("tensor") / basis.shape[1])
    momentum, *rest = main(grad, momentum, basis)
    return finish(scale, momentum, *rest)


def solution(mesh):
    return jax.shard_map(
        on_device,
        mesh=mesh,
        in_specs=(P("fsdp", "tensor"), P("fsdp", "tensor"), P("tensor", None)),
        out_specs=(P("fsdp", "tensor"), P("fsdp", "tensor"), P("tensor", None)),
        check_vma=False,
    )
```

```python
import functools
import math

import jax
import jax.numpy as jnp
from jax import lax
from jax.experimental import pallas as pl
from jax.experimental.pallas import tpu as pltpu
from jax.sharding import PartitionSpec as P

MESH = pl.DeviceIdType.MESH
BF16 = jnp.bfloat16
HIGH = lax.Precision.HIGHEST
F32 = jnp.float32


def dot(a, b, dims):
    return lax.dot_general(a, b, (dims, ((), ())), precision=HIGH, preferred_element_type=F32)


def inverse_factor(square):
    size = square.shape[0]
    tall = size // 8
    tiles = [square[8 * i : 8 * i + 8, :] for i in range(tall)]
    lane = lax.broadcasted_iota(jnp.int32, (8, size), 1)
    sub = lax.broadcasted_iota(jnp.int32, (8, size), 0)
    pivots = []
    for t in range(tall):
        start = 8 * t
        left = tall - t
        cols = [
            [jnp.broadcast_to(tiles[i][:, start + l : start + l + 1], (8, size)) for i in range(t, tall)]
            for l in range(8)
        ]
        mult = [[None] * left for _ in range(8)]
        group = tiles[t]
        rows = []
        pivot = jnp.zeros((8, size), F32)
        for l in range(8):
            here = cols[l][0][l : l + 1, :]
            recip = jnp.broadcast_to(1.0 / here, (8, size))
            pivot = jnp.where(sub == l, here, pivot)
            mult[l][0] = jnp.where(sub > l, cols[l][0] * recip, 0.0)
            for i in range(1, left):
                mult[l][i] = cols[l][i] * recip
            for later in range(l + 1, 8):
                across = jnp.broadcast_to(cols[later][0][l : l + 1, :], (8, size))
                for i in range(left):
                    cols[later][i] = cols[later][i] - mult[l][i] * across
            at = start + l
            row = jnp.where(lane[:1] == at, 1.0, group[l : l + 1, :])
            group = jnp.where((lane == at) & (sub > l), 0.0, group)
            group = group - mult[l][0] * jnp.broadcast_to(row, (8, size))
            row = jnp.where((lane[:1] > at) & (lane[:1] < start + 8), 0.0, row)
            rows.append(jnp.broadcast_to(row, (8, size)))
        tiles[t] = group
        pivots.append(pivot)
        for i in range(1, left):
            total = mult[0][i] * rows[0]
            for l in range(1, 8):
                total = total + mult[l][i] * rows[l]
            kept = jnp.where((lane >= start) & (lane < start + 8), 0.0, tiles[t + i])
            tiles[t + i] = kept - total
    out = []
    for i in range(tall):
        at = sub + 8 * i
        unit = jnp.where(lane == at, 1.0, jnp.where(lane < at, tiles[i], 0.0))
        out.append(unit * lax.rsqrt(pivots[i]))
    return jnp.concatenate(out, 0)


def factor_kernel(gram_ref, out_ref):
    half = gram_ref.shape[0] // 2
    first = inverse_factor(gram_ref[:half, :half])
    across = dot(first, gram_ref[:half, half:], ((1,), (0,)))
    second = inverse_factor(gram_ref[half:, half:] - dot(across, across, ((0,), (0,))))
    below = -dot(across, first, ((0,), (0,)))
    out_ref[:half, :half] = first
    out_ref[:half, half:] = jnp.zeros((half, half), F32)
    out_ref[half:, :half] = dot(second, below, ((1,), (0,)))
    out_ref[half:, half:] = second


def fast_dot(a, b, dims):
    return lax.dot_general(a, b, (dims, ((), ())), preferred_element_type=F32)


def two_parts(value):
    upper = value.astype(BF16)
    return upper, (value - upper.astype(F32)).astype(BF16)


def put(src, dst, send, recv, **where):
    copy = pltpu.make_async_remote_copy(
        src_ref=src, dst_ref=dst, send_sem=send, recv_sem=recv, device_id=where, device_id_type=MESH
    )
    copy.start()
    return copy


def place():
    flat = lax.axis_index("fsdp")
    return flat // 8, flat % 8 // 2, flat % 2, lax.axis_index("tensor")


def at(z, x, core):
    return z * 8 + x * 2 + core


def greet(others):
    barrier = pltpu.get_barrier_semaphore()
    for where in others:
        pl.semaphore_signal(barrier, inc=1, device_id=where, device_id_type=MESH)
    return lambda: pl.semaphore_wait(barrier, len(others))


ORDER = (2, 1, 3, 0)
ALONG_YX = tuple(
    sorted(
        ((oy, ox) for oy in range(4) for ox in range(4) if oy or ox),
        key=lambda o: -min(o[0], 4 - o[0]) - min(o[1], 4 - o[1]),
    )
)
ALONG_Z = (4, 3, 5, 2, 6, 1, 7)


def main_kernel(
    grad_hbm, momentum_hbm, basis_hbm,
    new_momentum, rounded, ortho, ortho_low, scales,
    grad_in, momentum_in, basis_in, high, low, high_turned, low_turned, piece, piece_sent, panel_got, panel, panel_own, panel_there,
    gram_own, gram_half, gram_got, gram_z, gram, inverse,
    cross, cross_got, lane_sent, lane_got, block, block_got, squares, squares_z, halves,
    load_sem, ysend, yrecv, gsend, grecv, zgsend, zgrecv, g2send, g2recv, g3send, g3recv,
    csend, crecv, xsend, xrecv, zsend, zrecv, azsend, azrecv, axsend, axrecv, acsend, acrecv, sqsend, sqrecv, sqzsend, sqzrecv,
):
    z, x, core, y = place()
    rows = grad_hbm.shape[0]
    fourth = rows // 4
    taller = fourth + 8
    sibling = at(z, x, 1 - core)
    across_z = [{"fsdp": at((z + o) % 8, x, core)} for o in ALONG_Z]
    others = across_z + [{"tensor": (y + o) % 4} for o in (2, 1, 3)]
    others += [{"fsdp": at(z, (x + o) % 4, core)} for o in (2, 1, 3)]
    others += [{"fsdp": sibling}]
    greeted = greet(others)
    basis_load = pltpu.make_async_copy(basis_hbm, basis_in, load_sem.at[8])
    basis_load.start()
    loads = []
    for n, o in enumerate(ORDER):
        p = (y + o) % 4
        start = pl.multiple_of(p * fourth - 8 * (p % 2), 16)
        for which, (src, dst) in enumerate(((grad_hbm, grad_in), (momentum_hbm, momentum_in))):
            load = pltpu.make_async_copy(src.at[pl.ds(start, taller)], dst.at[n], load_sem.at[2 * n + which])
            load.start()
            loads.append(load)
    basis_load.wait()
    sent = []

    def send(src, dst, send_sem, recv_sem, **where):
        copy = put(src, dst, send_sem, recv_sem, **where)
        sent.append(copy)
        return copy

    copies = []
    for n, o in enumerate(ORDER):
        p = (y + o) % 4
        start = pl.multiple_of(p * fourth - 8 * (p % 2), 16)
        skip = pl.multiple_of(8 * (p % 2), 8)
        loads[2 * n].wait()
        loads[2 * n + 1].wait()
        upper, lower = two_parts(momentum_in[n] + grad_in[n].astype(F32))
        high[pl.ds(start, taller), :] = upper
        low[pl.ds(start, taller), :] = lower
        basis_v = basis_in[...]
        piece[n] = fast_dot(upper, basis_v, ((1,), (0,))) + fast_dot(lower, basis_v, ((1,), (0,)))
        if n == 0:
            greeted()
        if o:
            piece_sent[n] = piece[n].astype(BF16)
            copies.append(send(piece_sent.at[n], panel_got.at[o - 1], ysend.at[o - 1], yrecv.at[o - 1], tensor=p))
    for n in range(8):
        wide = slice(256 * n, 256 * n + 256)
        high_turned[wide, :] = high[:, wide].T
        low_turned[wide, :] = low[:, wide].T
    skip = pl.multiple_of(8 * (y % 2), 8)
    for copy in copies:
        copy.wait_recv()
    for o in (1, 2, 3):
        piece[3] = piece[3] + panel_got[o - 1].astype(F32)
    total = piece[3, pl.ds(skip, fourth), :]
    mine = pl.ds(pl.multiple_of(y * fourth, 8), fourth)
    panel_own[...] = jnp.concatenate([total, jnp.zeros((8, total.shape[1]), F32)], 0).astype(BF16)
    gathers = [
        send(panel_own, panel_there.at[o - 1], ysend.at[2 + o], yrecv.at[2 + o], tensor=(y + o) % 4) for o in (1, 2, 3)
    ]

    half = 128
    panel[mine, :] = panel_own[...].astype(F32)[:fourth]
    gram_own[...] = fast_dot(panel_own[...], panel_own[...], ((0,), (0,)))
    away = send(gram_own.at[pl.ds(pl.multiple_of((1 - core) * half, half), half)], gram_half, g3send.at[0], g3recv.at[0], fsdp=sibling)
    away.wait_recv()
    kept = pl.ds(pl.multiple_of(core * half, half), half)
    gram_half[...] = gram_half[...] + gram_own[kept, :]
    spread = []
    for n, (oy, ox) in enumerate(ALONG_YX):
        ty, tx = (y + oy) % 4, (x + ox) % 4
        src = gram_half.at[pl.ds(pl.multiple_of((ty * 4 + tx) * 8, 8), 8)]
        spread.append(send(src, gram_got.at[n], gsend.at[n], grecv.at[n], fsdp=at(z, tx, core), tensor=ty))
    for copy in gathers:
        copy.wait_recv()
    for o in (1, 2, 3):
        panel[pl.ds(pl.multiple_of((y + 4 - o) % 4 * fourth, 8), fourth), :] = panel_there[o - 1].astype(F32)[:fourth]
    panel_high = panel[...].astype(BF16)

    def product(start):
        upper = high_turned[pl.ds(pl.multiple_of(start, 256), 256), :]
        lower = low_turned[pl.ds(pl.multiple_of(start, 256), 256), :]
        return (
            fast_dot(upper, panel_high, ((1,), (0,)))
            + fast_dot(lower, panel_high, ((1,), (0,)))
        )

    crossing = []
    for n, o in enumerate(ORDER):
        cross[n] = product((1 - core) * 1024 + (x + o) % 4 * 256)
        crossing.append(send(cross.at[n], cross_got.at[n], csend.at[n], crecv.at[n], fsdp=sibling))
    passing = []
    for n, o in ((0, 2), (1, 1)):
        own = product(core * 1024 + (x + o) % 4 * 256)
        crossing[n].wait_recv()
        own = own + cross_got[n]
        if o:
            lane_sent[n] = own.astype(BF16)
            passing.append(
                send(lane_sent.at[n], lane_got.at[o - 1], xsend.at[o - 1], xrecv.at[o - 1], fsdp=at(z, (x + o) % 4, core))
            )
        else:
            block[...] = own
    for copy in spread:
        copy.wait_recv()
    eight = (y * 4 + x) * 8
    total = gram_half[pl.ds(pl.multiple_of(eight, 8), 8), :]
    for n in range(15):
        total = total + gram_got[n]
    gram_z[z] = total
    around = [
        send(gram_z.at[z], gram_z.at[z], zgsend.at[o - 1], zgrecv.at[o - 1], fsdp=at((z + o) % 8, x, core))
        for o in ALONG_Z
    ]
    for n, o in ((2, 3), (3, 0)):
        own = product(core * 1024 + (x + o) % 4 * 256)
        crossing[n].wait_recv()
        own = own + cross_got[n]
        if o:
            lane_sent[n] = own.astype(BF16)
            passing.append(
                send(lane_sent.at[n], lane_got.at[o - 1], xsend.at[o - 1], xrecv.at[o - 1], fsdp=at(z, (x + o) % 4, core))
            )
        else:
            block[...] = own

    for copy in around:
        copy.wait_recv()
    total = gram_z[0]
    for n in range(1, 8):
        total = total + gram_z[n]
    here = pl.ds(pl.multiple_of(core * half + eight, 8), 8)
    gram[here, :] = total
    spread = [
        send(gram.at[here], gram.at[here], g2send.at[n], g2recv.at[n], fsdp=at(z, (x + ox) % 4, core), tensor=(y + oy) % 4)
        for n, (oy, ox) in enumerate(ALONG_YX)
    ]
    for copy in spread:
        copy.wait_recv()
    away = send(gram.at[kept], gram.at[kept], g3send.at[1], g3recv.at[1], fsdp=sibling)

    for copy in passing:
        copy.wait_recv()
    block[...] = block[...] + lane_got[0].astype(F32) + lane_got[1].astype(F32) + lane_got[2].astype(F32)
    last = []
    for o in ALONG_Z:
        to = (z + o) % 8
        last.append(
            send(block.at[pl.ds(pl.multiple_of(to * 32, 32), 32)], block_got.at[o - 1], zsend.at[o - 1], zrecv.at[o - 1],
                 fsdp=at(to, x, core))
        )
    away.wait_recv()
    factor_kernel(gram, inverse)
    for copy in last:
        copy.wait_recv()
    total = block[pl.ds(pl.multiple_of(z * 32, 32), 32), :]
    for n in range(7):
        total = total + block_got[n]

    def rows_of(z_of):
        return pl.ds(pl.multiple_of(core * 1024 + x * 256 + z_of * 32, 32), 32)

    here = rows_of(z)
    own = dot(total, inverse[...], ((1,), (1,))).astype(BF16)
    rounded[here, :] = own
    along_z = [
        send(rounded.at[here], rounded.at[here], azsend.at[o - 1], azrecv.at[o - 1], fsdp=at((z + o) % 8, x, core))
        for o in range(1, 8)
    ]
    along_x = [[None] * 8 for _ in range(4)]

    def pass_on(zo):
        here = rows_of((z + 8 - zo) % 8)
        for o in (2, 1, 3):
            along_x[o][zo] = send(
                rounded.at[here], rounded.at[here], axsend.at[o - 1, zo], axrecv.at[o - 1, zo], fsdp=at(z, (x + o) % 4, core)
            )

    pass_on(0)
    own = own.astype(F32)
    slot = y * 4 + x
    squares[slot] = jnp.sum(own * own, axis=0, keepdims=True)
    spread = [
        send(squares.at[slot], squares.at[slot], sqsend.at[n], sqrecv.at[n], fsdp=at(z, (x + ox) % 4, core), tensor=(y + oy) % 4)
        for n, (oy, ox) in enumerate(ALONG_YX)
    ]
    upper, lower = two_parts(dot(panel[...], inverse[...], ((1,), (1,))))
    ortho[...] = upper
    ortho_low[...] = lower
    for zo in (1, 7, 2, 6, 3, 5):
        along_z[zo - 1].wait_recv()
        pass_on(zo)
    for copy in spread:
        copy.wait_recv()
    total = squares[0]
    for n in range(1, 16):
        total = total + squares[n]
    squares_z[z] = total
    around = [
        send(squares_z.at[z], squares_z.at[z], sqzsend.at[o - 1], sqzrecv.at[o - 1], fsdp=at((z + o) % 8, x, core))
        for o in ALONG_Z
    ]
    along_z[3].wait_recv()
    pass_on(4)

    def block_of(o):
        return pl.ds(pl.multiple_of(core * 1024 + (x + 4 - o) % 4 * 256, 256), 256)

    def block_there(o):
        return pl.ds(pl.multiple_of((1 - core) * 1024 + (x + 4 - o) % 4 * 256, 256), 256)

    def feed_back(span):
        back = fast_dot(ortho[...], rounded[span, :], ((1,), (1,)))
        new_momentum[:, span] = high[:, span].astype(F32) + low[:, span].astype(F32) - 0.05 * back

    across = [send(rounded.at[block_of(0)], rounded.at[block_of(0)], acsend.at[0], acrecv.at[0], fsdp=sibling)]
    feed_back(block_of(0))
    across[0].wait_recv()
    feed_back(block_there(0))
    for n, o in enumerate((1, 3, 2)):
        for copy in along_x[o]:
            copy.wait_recv()
        across.append(send(rounded.at[block_of(o)], rounded.at[block_of(o)], acsend.at[o], acrecv.at[o], fsdp=sibling))
        feed_back(block_of(o))
        if n < 2:
            across[-1].wait_recv()
            feed_back(block_there(o))
    for copy in around:
        copy.wait_recv()
    total = squares_z[0]
    for n in range(1, 8):
        total = total + squares_z[n]
    halves[core] = total
    away = send(halves.at[core], halves.at[core], g3send.at[2], g3recv.at[2], fsdp=sibling)
    across[-1].wait_recv()
    feed_back(block_there(2))
    away.wait_recv()
    total = halves[0] + halves[1]
    scales[...] = jnp.broadcast_to(lax.rsqrt(total + 1e-06), scales.shape)
    for copy in sent:
        copy.wait_send()


def main(grad, momentum, basis):
    rows, cols = grad.shape
    rank = basis.shape[1]
    fourth = rows // 4
    dma = pltpu.SemaphoreType.DMA
    vmem = pltpu.VMEM
    pairs = ((6,), (15,), (7,), (15,), (3,), (4,), (3,), (7,), (7,), (3, 8), (4,), (15,), (7,))
    return pl.pallas_call(
        main_kernel,
        out_shape=(
            jax.ShapeDtypeStruct((rows, cols), F32),
            jax.ShapeDtypeStruct((cols, rank), BF16),
            jax.ShapeDtypeStruct((rows, rank), BF16),
            jax.ShapeDtypeStruct((rows, rank), BF16),
            jax.ShapeDtypeStruct((8, rank), F32),
        ),
        in_specs=[pl.BlockSpec(memory_space=pltpu.HBM)] * 3,
        out_specs=(pl.BlockSpec(memory_space=pltpu.VMEM),) * 5,
        scratch_shapes=[
            vmem((4, fourth + 8, cols), BF16),
            vmem((4, fourth + 8, cols), F32),
            vmem((cols, rank), BF16),
            vmem((rows, cols), BF16),
            vmem((rows, cols), BF16),
            vmem((cols, rows), BF16),
            vmem((cols, rows), BF16),
            vmem((4, fourth + 8, rank), F32),
            vmem((3, fourth + 8, rank), BF16),
            vmem((3, fourth + 8, rank), BF16),
            vmem((rows, rank), F32),
            vmem((fourth + 8, rank), BF16),
            vmem((3, fourth + 8, rank), BF16),
            vmem((rank, rank), F32),
            vmem((rank // 2, rank), F32),
            vmem((15, 8, rank), F32),
            vmem((8, 8, rank), F32),
            vmem((rank, rank), F32),
            vmem((rank, rank), F32),
            vmem((4, 256, rank), F32),
            vmem((4, 256, rank), F32),
            vmem((3, 256, rank), BF16),
            vmem((3, 256, rank), BF16),
            vmem((256, rank), F32),
            vmem((7, 32, rank), F32),
            vmem((16, 1, rank), F32),
            vmem((8, 1, rank), F32),
            vmem((2, 1, rank), F32),
            dma((9,)),
            *[dma(shape) for shape in pairs for _ in range(2)],
        ],
        compiler_params=pltpu.CompilerParams(collective_id=0, has_side_effects=True, vmem_limit_bytes=40 << 20),
    )(*[pltpu.with_memory_space_constraint(v, pltpu.HBM) for v in (grad, momentum, basis)])


def finish_kernel(scale, momentum, rounded, ortho, ortho_low, scales, new_momentum, update, basis_next, part, following, sems):
    wide = 512
    many = rounded.shape[0] // wide
    tall = momentum.shape[0] // many
    copies = []
    for n in range(many):
        span = pl.ds(n * tall, tall)
        copies.append(pltpu.make_async_copy(momentum.at[span], new_momentum.at[span], sems.at[2 * many + n]))
        copies[-1].start()
    for n in range(many):
        span = pl.ds(n * wide, wide)
        block = (rounded[span, :].astype(F32) * scales[:1, :]).astype(BF16)
        following[span, :] = block
        step = fast_dot(ortho[...], block, ((1,), (1,))) + fast_dot(ortho_low[...], block, ((1,), (1,)))
        part[n] = (scale * step).astype(BF16)
        copies.append(pltpu.make_async_copy(following.at[span], basis_next.at[span], sems.at[2 * n]))
        copies.append(pltpu.make_async_copy(part.at[n], update.at[:, span], sems.at[2 * n + 1]))
        copies[-2].start()
        copies[-1].start()
    for copy in copies:
        copy.wait()


def finish(scale, momentum, rounded, ortho, ortho_low, scales):
    rows, cols = momentum.shape
    rank = ortho.shape[1]
    return pl.pallas_call(
        functools.partial(finish_kernel, scale),
        out_shape=(
            jax.ShapeDtypeStruct((rows, cols), F32),
            jax.ShapeDtypeStruct((rows, cols), BF16),
            jax.ShapeDtypeStruct((cols, rank), BF16),
        ),
        in_specs=[pl.BlockSpec(memory_space=pl.ANY)] + [pl.BlockSpec(memory_space=pltpu.VMEM)] * 4,
        out_specs=(pl.BlockSpec(memory_space=pl.ANY),) * 3,
        scratch_shapes=[
            pltpu.VMEM((cols // 512, rows, 512), BF16),
            pltpu.VMEM((cols, rank), BF16),
            pltpu.SemaphoreType.DMA((3 * cols // 512,)),
        ],
        compiler_params=pltpu.CompilerParams(vmem_limit_bytes=16 << 20),
    )(momentum, rounded, ortho, ortho_low, scales)


def on_device(grad, momentum, basis):
    rows_here, cols_here = grad.shape
    scale = math.sqrt(rows_here * lax.axis_size("fsdp") * cols_here * lax.axis_size("tensor") / basis.shape[1])
    momentum, *rest = main(grad, momentum, basis)
    return finish(scale, momentum, *rest)


def solution(mesh):
    return jax.shard_map(
        on_device,
        mesh=mesh,
        in_specs=(P("fsdp", "tensor"), P("fsdp", "tensor"), P("tensor", None)),
        out_specs=(P("fsdp", "tensor"), P("fsdp", "tensor"), P("tensor", None)),
        check_vma=False,
    )
```
